256 devices in a mesh: zone: 64 (over y, z, core), ja: 4 (over x).
Axes of the slice: x: 4, y: 4, z: 8, core: 2. Of those that a mesh axis runs over, the one named last changes fastest.
Arguments:
- flow_state: float32 [64, 32, 5, 16, 128], P('zone', 'ja'), may hold values from -3 to 3
- forcing: float32 [64, 32, 5, 16, 128], P('zone', 'ja'), may hold values from -6 to 6
- diag_block: float32 [64, 32, 5, 5, 16, 128], P('zone', 'ja'), may hold values from -0.4 to 7.2
- lower_jac: float32 [64, 32, 5, 5, 16, 128], P('zone', 'ja'), may hold values from -4.9 to 0.2
- upper_jac: float32 [64, 32, 5, 5, 16, 128], P('zone', 'ja'), may hold values from -4.9 to 0.2
- block_inv: float32 [64, 32, 5, 5, 16, 128], P('zone', 'ja'), may hold values from -0.03 to 0.21
- east_zone: int32 [64], replicated, may hold values from 0 to 63, each once
- zone_depth: int32 [64], replicated, may hold values from 4 to 16, as said below
Outputs:
- new_state: float32 [64, 32, 5, 16, 128], P('zone', 'ja')
- last_residual: float32 [64, 32, 5, 16, 128], P('zone', 'ja')
The draws below stay inside these ranges and needn't reach their ends.
Inputs may be any that keep to these rules, and one draw needn't show every extreme that they name: `east_zone`: a permutation of the zones. `zone_depth`: some zone has all 16 planes live.
All inputs are finite; a program needn't handle non-finite values.
Results may differ from the reference program's by a relative error of at most 0.0003.
Values sent between devices are 32-bit elements; how exact they have to be, the bound alone decides.
A program may use at most 64 MiB of HBM per device.

```python
import math
import jax
import jax.numpy as jnp
from jax import lax

NVAR = 5
KC = 16
IC = 128
ITERS = 2
ZONES = 64
JZ = 32


def block_field(key, diag_lo, diag_hi, rough, off_scale):
    shape = (ZONES, JZ, 5, 5, KC, IC)
    key_base, key_rough, key_off = jax.random.split(key, 3)
    base = jnp.exp(jax.random.uniform(key_base, (ZONES, 1, 5, 1, 1, 1), jnp.float32, math.log(diag_lo), math.log(diag_hi)))
    roughness = jax.random.uniform(key_rough, shape, jnp.float32, 1.0 - rough, 1.0 + rough)
    noise = off_scale * jax.random.uniform(key_off, shape, jnp.float32, -1.0, 1.0)
    identity = jnp.eye(5, dtype=jnp.float32).reshape(1, 1, 5, 5, 1, 1)
    return identity * base * roughness + (1.0 - identity) * noise


def draw_diag_block(key, part):
    return block_field(jax.random.fold_in(key, 11), 5.0, 6.5, 0.1, 0.4)


def draw_lower_jac(key, part):
    return -block_field(jax.random.fold_in(key, 12), 4.0, 4.4, 0.1, 0.2)


def draw_upper_jac(key, part):
    return -block_field(jax.random.fold_in(key, 13), 4.0, 4.4, 0.1, 0.2)


def draw_block_inv(key, part):
    return block_field(jax.random.fold_in(key, 14), 0.15, 0.19, 0.1, 0.03)


def draw_zone_depth(key, part):
    key_depth, key_full = jax.random.split(jax.random.fold_in(key, 7))
    lowest = max(1, KC // 4)
    depths = jax.random.randint(key_depth, (ZONES,), lowest, KC + 1, dtype=jnp.int32)
    full_zone = jax.random.randint(key_full, (), 0, ZONES, dtype=jnp.int32)
    return jnp.where(jnp.arange(ZONES, dtype=jnp.int32) == full_zone, KC, depths).astype(jnp.int32)


def block_scale(rng, extent, cuts, smallest, high):
    level, own = 1.0, jax.random.fold_in(rng, 6)
    for position, shards_of in cuts:
        draws = jnp.exp(jax.random.uniform(jax.random.fold_in(own, position), (shards_of,), jnp.float32, smallest / len(cuts), high / len(cuts)))
        level = level * jnp.repeat(draws, extent[position] // shards_of).reshape([-1 if axis == position else 1 for axis in range(len(extent))])
    return level


def bell_draw(rng, dims, deviation, limit, pieces=(), kind=jnp.bfloat16):
    result = jax.random.normal(rng, dims, jnp.float32) * deviation
    if len(pieces) > 0:
        result = block_scale(rng, dims, pieces, -0.22, 0.18) * result
    return jnp.clip(result, min=-limit, max=limit).astype(kind)


def setup_inputs(seed: int = 0) -> dict:
    keys = jax.random.split(jax.random.key(seed), 9)
    return {
        "flow_state": bell_draw(keys[0], (ZONES, JZ, NVAR, KC, IC), 0.3, 3.0, ((0, 64), (1, 4)), jnp.float32),
        "forcing": bell_draw(keys[1], (ZONES, JZ, NVAR, KC, IC), 1.0, 6.0, ((0, 64), (1, 4)), jnp.float32),
        "diag_block": draw_diag_block(jax.random.fold_in(keys[8], 71), 0),
        "lower_jac": draw_lower_jac(jax.random.fold_in(keys[8], 71), 0),
        "upper_jac": draw_upper_jac(jax.random.fold_in(keys[8], 71), 0),
        "block_inv": draw_block_inv(jax.random.fold_in(keys[8], 71), 0),
        "east_zone": jax.random.permutation(keys[6], ZONES).astype(jnp.int32),
        "zone_depth": draw_zone_depth(jax.random.fold_in(keys[8], 71), 0),
    }


OMEGA = 1.2
COUPLE = 0.25


def matvec(matrix, vector):
    return jnp.sum(matrix * vector[..., None, :, :, :], axis=-3)


def zone_update(inputs):
    current, forcing, diag_block, lower_jac, upper_jac, block_inv, ghost_low, ghost_high, live_count = inputs
    k_index = jnp.arange(current.shape[2], dtype=jnp.int32)
    live_mask = (k_index < live_count).astype(jnp.float32)[None, None, :, None]
    zero_j = jnp.zeros_like(current[:1])
    below_j = jnp.concatenate([zero_j, current[:-1]], axis=0)
    above_j = jnp.concatenate([current[1:], zero_j], axis=0)
    left_i = jnp.concatenate([ghost_low[..., None], current[..., :-1]], axis=3)
    right_i = jnp.concatenate([current[..., 1:], ghost_high[..., None]], axis=3)
    zero_k = jnp.zeros_like(current[:, :, :1])
    down_k = jnp.concatenate([zero_k, current[:, :, :-1]], axis=2)
    up_k = jnp.concatenate([current[:, :, 1:], zero_k], axis=2)
    applied = matvec(diag_block, current) - matvec(lower_jac, below_j) - matvec(upper_jac, above_j) - COUPLE * (left_i + right_i + down_k + up_k)
    residual = live_mask * (forcing - applied)

    def lower_step(previous, planes):
        res_plane, inv_plane, jac_plane = planes
        value = matvec(inv_plane, res_plane + OMEGA * matvec(jac_plane, previous))
        return value, value

    no_inflow = jnp.zeros_like(residual[0])
    _, lowered = lax.scan(lower_step, no_inflow, (residual, block_inv, lower_jac))

    def upper_step(following, planes):
        low_plane, inv_plane, jac_plane = planes
        value = low_plane + OMEGA * matvec(inv_plane, matvec(jac_plane, following))
        return value, value

    _, raised = lax.scan(upper_step, no_inflow, (lowered, block_inv, upper_jac), reverse=True)
    return current + raised, residual


def reference(flow_state, forcing, diag_block, lower_jac, upper_jac, block_inv, east_zone, zone_depth):
    k_index = jnp.arange(KC, dtype=jnp.int32)
    live_mask = (k_index[None, :] < zone_depth[:, None]).astype(jnp.float32)
    current = flow_state * live_mask[:, None, None, :, None]
    west_zone = jnp.zeros((ZONES,), jnp.int32).at[east_zone].set(jnp.arange(ZONES, dtype=jnp.int32))
    residual = jnp.zeros_like(current)
    for iteration in range(ITERS):
        low_faces = current[..., 0]
        high_faces = current[..., -1]
        ghost_high = low_faces[east_zone]
        ghost_low = high_faces[west_zone]
        current, residual = lax.map(zone_update, (current, forcing, diag_block, lower_jac, upper_jac, block_inv, ghost_low, ghost_high, zone_depth))
    return current, residual
```

```python
import functools

import jax
import jax.numpy as jnp
from jax import lax
from jax.experimental import pallas as pl
from jax.experimental.pallas import tpu as pltpu
from jax.sharding import PartitionSpec as P

ITERS = 2
OMEGA = 1.2
COUPLE = 0.25
NY, NZ, NX = 4, 8, 4
MESH = pl.DeviceIdType.MESH
F32 = jnp.float32


def kernel(
    east_ref, depth_ref, flow_hbm, forc_hbm, diag_hbm, low_hbm, upp_hbm, inv_hbm,
    state_hbm, resid_hbm,
    cur, forc, diag, low, upp, inv, mm, nn, res, swp,
    mine_a, mine_b, got_a, got_b,
    gz_first, gz_second, qs, gq, halo, sb, sc, bx, cy, inflow,
    load_sem, bar_z_s, bar_z_r, sib_s, sib_r, y_s, y_r, halo_s, halo_r,
    a_s, a_r, b_s, b_r, x_s, x_r, u_s, u_r, out_sem,
):
    planes, nvar, depth_k, width = cur.shape
    rows = nvar * depth_k
    zone = lax.axis_index("zone")
    ja = lax.axis_index("ja")
    y, z, c = zone // (2 * NZ), (zone // 2) % NZ, zone % 2

    def at(dy, dz, flip):
        core = 1 - c if flip else c
        return (((y + dy) % NY) * (2 * NZ) + ((z + dz) % NZ) * 2 + core, ja)

    def along(dx):
        return (zone, (ja + dx) % NX)

    gz = (gz_first, gz_second)
    far_z = (4, 3, 5, 2, 6, 1, 7)
    far_y = (2, 1, 3)
    far_x = (2, 1, 3)
    barrier = pltpu.get_barrier_semaphore()
    partners = [at(0, d, False) for d in far_z] + [at(d, 0, False) for d in far_y]
    partners += [along(d) for d in far_x] + [at(0, 0, True)]
    for partner in partners:
        pl.semaphore_signal(barrier, 1, device_id=partner, device_id_type=MESH)

    sources = ((flow_hbm, cur), (inv_hbm, inv), (low_hbm, low), (upp_hbm, upp), (forc_hbm, forc), (diag_hbm, diag))
    loads = [pltpu.make_async_copy(src, dst, load_sem.at[i]) for i, (src, dst) in enumerate(sources)]
    for load in loads:
        load.start()

    targets = [at(d, 0, False)[0] for d in range(NY)]

    def find(w, found):
        e = east_ref[w]
        return tuple(jnp.where(e == t, w, f) for t, f in zip(targets, found))

    wests = lax.fori_loop(0, east_ref.shape[0], find, (jnp.int32(0),) * NY)
    easts = [east_ref[t] for t in targets]

    k_index = lax.broadcasted_iota(jnp.int32, (depth_k, width), 0)
    lane = lax.broadcasted_iota(jnp.int32, (depth_k, width), 1)
    live = (k_index < depth_ref[zone]).astype(F32)
    edge = ((lane == 0) | (lane == width - 1)).astype(F32)
    left_ok = (lane > 0).astype(F32)
    right_ok = (lane < width - 1).astype(F32)
    down_ok = (k_index > 0).astype(F32)
    up_ok = (k_index < depth_k - 1).astype(F32)

    def matvec(ref, j, v):
        out = ref[j, :, 0] * v[0][None]
        for col in range(1, nvar):
            out += ref[j, :, col] * v[col][None]
        return out

    def matmat(ref, j, other):
        return [matvec(ref, j, other[col]) for col in range(nvar)]

    def pack_faces(it):
        def step(m, packet):
            tile = cur[m // nvar, m % nvar]
            turned = pltpu.roll(tile, 2 * m + 1, 1)
            return jnp.where((lane == 2 * m) | (lane == 2 * m + 1), turned, packet)

        gz[it][c, z] = lax.fori_loop(0, planes * nvar, step, jnp.zeros((depth_k, width), F32))

    def z_copy(it, dz, incoming):
        slot = (z - dz) % NZ if incoming else z
        return pltpu.make_async_remote_copy(
            gz[it].at[c, z], gz[it].at[c, slot], bar_z_s.at[it, dz], bar_z_r.at[it, dz],
            device_id=at(0, dz, False), device_id_type=MESH)

    def sib_copy(it, incoming):
        side = 1 - c if incoming else c
        return pltpu.make_async_remote_copy(
            gz[it].at[c], gz[it].at[side], sib_s.at[it], sib_r.at[it],
            device_id=at(0, 0, True), device_id_type=MESH)

    def y_copy(it, dy):
        return pltpu.make_async_remote_copy(
            qs.at[it, dy], gq.at[it, dy], y_s.at[it, dy], y_r.at[it, dy],
            device_id=at(dy, 0, False), device_id_type=MESH)

    def choose(it):
        odd = lane % 2 == 1
        for dy in range(NY):
            w, e = wests[dy], easts[dy]
            west = gz[it][w % 2, (w // 2) % NZ]
            east = gz[it][e % 2, (e // 2) % NZ]
            west = jnp.where(w // (2 * NZ) == y, west, 0.0)
            east = jnp.where(e // (2 * NZ) == y, east, 0.0)
            qs[it, dy] = jnp.where(odd, pltpu.roll(west, 1, 1), pltpu.roll(east, width - 1, 1))
        for dy in far_y:
            y_copy(it, dy).start()

    def halo_copy(it, up):
        src = cur.at[0] if up else cur.at[planes - 1]
        side = 1 if up else 0
        return pltpu.make_async_remote_copy(
            src, halo.at[it, side], halo_s.at[it, side], halo_r.at[it, side],
            device_id=along(NX - 1 if up else 1), device_id_type=MESH)

    def matrix_copy(e, to, lower):
        mine, got, ss, rs = (mine_a, got_a, a_s, a_r) if lower else (mine_b, got_b, b_s, b_r)
        return pltpu.make_async_remote_copy(
            mine, got.at[e - 1], ss.at[to], rs.at[e - 1], device_id=(zone, jnp.int32(to)), device_id_type=MESH)

    def sweep_copy(it, source, to, lower):
        send, got, ss, rs = (sb, bx, x_s, x_r) if lower else (sc, cy, u_s, u_r)
        return pltpu.make_async_remote_copy(
            send.at[it], got.at[it, source], ss.at[it, to], rs.at[it, source],
            device_id=(zone, jnp.int32(to)), device_id_type=MESH)

    lower_pairs = [(0, 1), (0, 2), (0, 3), (1, 2), (1, 3), (2, 3)]
    upper_pairs = [(3, 0), (3, 1), (3, 2), (2, 1), (2, 0), (1, 0)]
    matrix_lower = [(1, 2), (1, 3), (2, 3)]
    matrix_upper = [(2, 1), (2, 0), (1, 0)]

    loads[0].wait()

    def mask_plane(j, carry):
        cur[j] = cur[j] * live[None]
        return carry

    lax.fori_loop(0, planes, mask_plane, 0)
    pack_faces(0)
    loads[1].wait()
    loads[2].wait()
    loads[3].wait()

    def premultiply(j, carry):
        for source, target in ((low, mm), (upp, nn)):
            for col in range(nvar):
                target[j, :, col] = OMEGA * matvec(inv, j, source[j, :, col])
        return carry

    lax.fori_loop(0, planes, premultiply, 0)
    mine_a[...] = mm[0]
    mine_b[...] = nn[planes - 1]

    def chain(s, carry):
        for col in range(nvar):
            mine_a[:, col] = matvec(mm, s, mine_a[:, col])
            mine_b[:, col] = matvec(nn, planes - 1 - s, mine_b[:, col])
        return carry

    lax.fori_loop(1, planes, chain, 0)
    loads[4].wait()
    loads[5].wait()
    pl.semaphore_wait(barrier, len(partners))

    for it in range(ITERS):
        if it > 0:
            pack_faces(it)
        for dz in far_z:
            z_copy(it, dz, False).start()

        @pl.when(ja > 0)
        def _():
            halo_copy(it, True).start()

        @pl.when(ja < NX - 1)
        def _():
            halo_copy(it, False).start()

        if it == 0:
            for lower, pairs in ((True, matrix_lower), (False, matrix_upper)):
                for e, to in pairs:
                    @pl.when(ja == e)
                    def _(e=e, to=to, lower=lower):
                        matrix_copy(e, to, lower).start()

        @pl.when(ja > 0)
        def _():
            halo_copy(it, False).wait_recv()

        @pl.when(ja == 0)
        def _():
            halo[it, 0] = jnp.zeros((nvar, depth_k, width), F32)

        @pl.when(ja < NX - 1)
        def _():
            halo_copy(it, True).wait_recv()

        @pl.when(ja == NX - 1)
        def _():
            halo[it, 1] = jnp.zeros((nvar, depth_k, width), F32)

        def residual(j, below):
            here = cur[j]
            above = jnp.where(j == planes - 1, halo[it, 1], cur[jnp.minimum(j + 1, planes - 1)])
            flat = here.reshape(rows, width)

            def shifted(by, axis, size, mask):
                return pltpu.roll(flat, by % size, axis).reshape(here.shape) * mask[None]

            beside = shifted(1, 1, width, left_ok) + shifted(-1, 1, width, right_ok)
            beside += shifted(1, 0, rows, down_ok) + shifted(-1, 0, rows, up_ok)
            applied = matvec(diag, j, here) - matvec(low, j, below) - matvec(upp, j, above) - COUPLE * beside
            res[j] = live[None] * (forc[j] - applied)
            return here

        lax.fori_loop(0, planes, residual, halo[it, 0])

        for dz in far_z:
            z_copy(it, dz, True).wait_recv()
        sib_copy(it, False).start()
        sib_copy(it, True).wait_recv()
        choose(it)
        for dy in far_y:
            y_copy(it, dy).wait_recv()
        ghosts = qs[it, 0] + gq[it, 1] + gq[it, 2] + gq[it, 3]
        ghost_weight = COUPLE * live * edge

        def add_ghost(m, carry):
            j, v = m // nvar, m % nvar
            res[j, v] += ghost_weight * pltpu.roll(ghosts, width - 1 - 2 * m, 1)
            return carry

        lax.fori_loop(0, planes * nvar, add_ghost, 0)
        if it == ITERS - 1:
            out_res = pltpu.make_async_copy(res, resid_hbm, out_sem.at[0])
            out_res.start()

        def solve(j, before):
            swp[j] = matvec(inv, j, res[j])
            swp[j] += matvec(mm, j, before)
            return swp[j]

        sb[it] = lax.fori_loop(0, planes, solve, jnp.zeros((nvar, depth_k, width), F32))
        for source, to in lower_pairs:
            @pl.when(ja == source)
            def _(source=source, to=to):
                sweep_copy(it, source, to, True).start()
        if it == 0:
            for lower, pairs in ((True, matrix_lower), (False, matrix_upper)):
                for e, to in pairs:
                    @pl.when(ja == to)
                    def _(e=e, to=to, lower=lower):
                        matrix_copy(e, to, lower).wait_recv()
        for source, to in lower_pairs:
            @pl.when(ja == to)
            def _(source=source, to=to):
                sweep_copy(it, source, to, True).wait_recv()

        @pl.when(ja == 0)
        def _():
            inflow[...] = jnp.zeros((nvar, depth_k, width), F32)

        @pl.when(ja > 0)
        def _():
            inflow[...] = bx[it, 0]

        for e in (1, 2):
            @pl.when(ja > e)
            def _(e=e):
                inflow[...] = bx[it, e] + matvec(got_a, e - 1, inflow[...])

        def lower_fix(j, change):
            change = matvec(mm, j, change)
            swp[j] += change
            return change

        lax.fori_loop(0, planes, lower_fix, inflow[...])

        def upper_step(s, after):
            j = planes - 1 - s
            swp[j] += matvec(nn, j, after)
            return swp[j]

        sc[it] = lax.fori_loop(0, planes, upper_step, jnp.zeros((nvar, depth_k, width), F32))
        for source, to in upper_pairs:
            @pl.when(ja == source)
            def _(source=source, to=to):
                sweep_copy(it, source, to, False).start()
        for source, to in upper_pairs:
            @pl.when(ja == to)
            def _(source=source, to=to):
                sweep_copy(it, source, to, False).wait_recv()

        @pl.when(ja == NX - 1)
        def _():
            inflow[...] = jnp.zeros((nvar, depth_k, width), F32)

        @pl.when(ja < NX - 1)
        def _():
            inflow[...] = cy[it, NX - 1]

        for e in (2, 1):
            @pl.when(ja < e)
            def _(e=e):
                inflow[...] = cy[it, e] + matvec(got_b, e - 1, inflow[...])

        @pl.when(ja > 0)
        def _():
            halo_copy(it, True).wait_send()

        @pl.when(ja < NX - 1)
        def _():
            halo_copy(it, False).wait_send()

        def upper_fix(s, change):
            j = planes - 1 - s
            change = matvec(nn, j, change)
            cur[j] += swp[j] + change
            return change

        lax.fori_loop(0, planes, upper_fix, inflow[...])

    out_state = pltpu.make_async_copy(cur, state_hbm, out_sem.at[1])
    out_state.start()
    for it in range(ITERS):
        for dz in far_z:
            z_copy(it, dz, False).wait_send()
        sib_copy(it, False).wait_send()
        for dy in far_y:
            y_copy(it, dy).wait_send()
        for lower, pairs in ((True, lower_pairs), (False, upper_pairs)):
            for source, to in pairs:
                @pl.when(ja == source)
                def _(source=source, to=to, lower=lower):
                    sweep_copy(it, source, to, lower).wait_send()
    for lower, pairs in ((True, matrix_lower), (False, matrix_upper)):
        for e, to in pairs:
            @pl.when(ja == e)
            def _(e=e, to=to, lower=lower):
                matrix_copy(e, to, lower).wait_send()
    out_res.wait()
    out_state.wait()


def per_device(flow_state, forcing, diag_block, lower_jac, upper_jac, block_inv, east_zone, zone_depth):
    planes, nvar, depth_k, width = flow_state.shape[1:]
    vec = (nvar, depth_k, width)
    mat = (nvar,) + vec
    dma = pltpu.SemaphoreType.DMA
    state, resid = pl.pallas_call(
        kernel,
        out_shape=[jax.ShapeDtypeStruct((planes,) + vec, F32)] * 2,
        in_specs=[pl.BlockSpec(memory_space=pltpu.SMEM)] * 2 + [pl.BlockSpec(memory_space=pl.ANY)] * 6,
        out_specs=[pl.BlockSpec(memory_space=pl.ANY)] * 2,
        scratch_shapes=[
            pltpu.VMEM((planes,) + vec, F32), pltpu.VMEM((planes,) + vec, F32),
            pltpu.VMEM((planes,) + mat, F32), pltpu.VMEM((planes,) + mat, F32),
            pltpu.VMEM((planes,) + mat, F32), pltpu.VMEM((planes,) + mat, F32),
            pltpu.VMEM((planes,) + mat, F32), pltpu.VMEM((planes,) + mat, F32),
            pltpu.VMEM((planes,) + vec, F32), pltpu.VMEM((planes,) + vec, F32),
            pltpu.VMEM(mat, F32), pltpu.VMEM(mat, F32),
            pltpu.VMEM((2,) + mat, F32), pltpu.VMEM((2,) + mat, F32),
            pltpu.VMEM((2, NZ, depth_k, width), F32), pltpu.VMEM((2, NZ, depth_k, width), F32),
            pltpu.VMEM((ITERS, NY, depth_k, width), F32), pltpu.VMEM((ITERS, NY, depth_k, width), F32),
            pltpu.VMEM((ITERS, 2) + vec, F32),
            pltpu.VMEM((ITERS,) + vec, F32), pltpu.VMEM((ITERS,) + vec, F32),
            pltpu.VMEM((ITERS, NX) + vec, F32), pltpu.VMEM((ITERS, NX) + vec, F32),
            pltpu.VMEM(vec, F32),
            dma((6,)), dma((ITERS, NZ)), dma((ITERS, NZ)), dma((ITERS,)), dma((ITERS,)),
            dma((ITERS, NY)), dma((ITERS, NY)), dma((ITERS, 2)), dma((ITERS, 2)),
            dma((NX,)), dma((2,)), dma((NX,)), dma((2,)),
            dma((ITERS, NX)), dma((ITERS, NX)), dma((ITERS, NX)), dma((ITERS, NX)), dma((2,)),
        ],
        compiler_params=pltpu.CompilerParams(
            collective_id=0, has_side_effects=True, vmem_limit_bytes=48 * 2**20),
        name="ssor",
    )(east_zone, zone_depth, flow_state[0], forcing[0], diag_block[0], lower_jac[0], upper_jac[0], block_inv[0])
    return state[None], resid[None]


def solution(mesh):
    vec = P("zone", "ja", None, None, None)
    mat = P("zone", "ja", None, None, None, None)
    return jax.shard_map(
        per_device,
        mesh=mesh,
        in_specs=(vec, vec, mat, mat, mat, mat, P(), P()),
        out_specs=(vec, vec),
        check_vma=False,
    )
```

```python
import jax
import jax.numpy as jnp
from jax import lax
from jax.experimental import pallas as pl
from jax.experimental.pallas import tpu as pltpu
from jax.sharding import PartitionSpec as P

ITERS = 2
OMEGA = 1.2
COUPLE = 0.25
NY, NZ, NX = 4, 8, 4
MESH = pl.DeviceIdType.MESH
F32 = jnp.float32
FACE_STEPS = ((2, 1), (2, 0), (1, 1), (3, 1), (1, 0), (3, 0), (0, 1))
Z_STEPS = (4, 3, 5, 2, 6, 1, 7)
JA_STEPS = (2, 1, 3)
LOWER_PAIRS = ((0, 2), (1, 3), (0, 1), (1, 2), (2, 3), (0, 3))
UPPER_PAIRS = ((3, 1), (2, 0), (3, 2), (2, 1), (1, 0), (3, 0))
LOWER_MATS = ((1, 2), (2, 3), (1, 3))
UPPER_MATS = ((2, 1), (1, 0), (2, 0))


def kernel(
    east_hbm, depth_hbm, flow_hbm, forc_hbm, diag_hbm, low_hbm, upp_hbm, inv_hbm,
    state_hbm, resid_hbm,
    east_ref, depth_ref, cur, forc, diag, low, upp, inv,
    mm, nn, pp, rr, hh, res, gres, sol, got_a, got_b,
    edge_pack, edge_mat, face0, face1, chosen, ghost_in, halo,
    sb, sc, bx, cy, xin, yin, small, small_vec,
    load_sem, face_s, face_r, z_s, z_r, halo_s, halo_r,
    a_s, a_r, b_s, b_r, e_s, e_r, x_s, x_r, u_s, u_r, g_s, g_r, out_sem,
):
    planes, nvar, depth_k, width = cur.shape
    rows = nvar * depth_k
    last = planes - 1
    vec = (nvar, depth_k, width)
    faces = (face0, face1)
    zone = lax.axis_index("zone")
    ja = lax.axis_index("ja")
    y, z, c = zone // (2 * NZ), (zone // 2) % NZ, zone % 2

    def at(dy, dz, flip):
        core = 1 - c if flip else c
        return (((y + dy) % NY) * (2 * NZ) + ((z + dz) % NZ) * 2 + core, ja)

    def along(dx):
        return (zone, (ja + dx) % NX)

    def on(device):
        return (zone, jnp.int32(device))

    barrier = pltpu.get_barrier_semaphore()
    partners = [at(dy, 0, flip) for dy, flip in FACE_STEPS] + [at(0, d, 0) for d in Z_STEPS]
    partners += [along(d) for d in JA_STEPS]
    for partner in partners:
        pl.semaphore_signal(barrier, 1, device_id=partner, device_id_type=MESH)

    sources = (
        (east_hbm, east_ref), (depth_hbm, depth_ref), (flow_hbm, cur), (inv_hbm, inv),
        (low_hbm, low), (upp_hbm, upp), (diag_hbm, diag), (forc_hbm, forc))
    loads = [pltpu.make_async_copy(src, dst, load_sem.at[i]) for i, (src, dst) in enumerate(sources)]
    for load in loads:
        load.start()

    k_index = lax.broadcasted_iota(jnp.int32, (depth_k, width), 0)
    lane = lax.broadcasted_iota(jnp.int32, (depth_k, width), 1)
    edge = ((lane == 0) | (lane == width - 1)).astype(F32)
    left_ok = (lane > 0).astype(F32)
    right_ok = (lane < width - 1).astype(F32)
    down_ok = (k_index > 0).astype(F32)
    up_ok = (k_index < depth_k - 1).astype(F32)
    odd = lane % 2 == 1

    def remote(src, dst, ss, rs, device):
        return pltpu.make_async_remote_copy(src, dst, ss, rs, device_id=device, device_id_type=MESH)

    def times(mat, v):
        out = mat[:, 0] * v[0][None]
        for col in range(1, nvar):
            out += mat[:, col] * v[col][None]
        return out

    def pack(tile, m, packet):
        turned = pltpu.roll(tile, 2 * m + 1, 1)
        return jnp.where((lane == 2 * m) | (lane == 2 * m + 1), turned, packet)

    def unpack(packet, m):
        return pltpu.roll(packet, width - 1 - 2 * m, 1)

    def pack_faces(it):
        packet = jnp.zeros((depth_k, width), F32)
        for m in range(planes * nvar):
            packet = pack(cur[m // nvar, m % nvar], m, packet)
        faces[it][c, y] = packet

    def face_copy(it, i, incoming):
        dy, flip = FACE_STEPS[i]
        slot = faces[it].at[1 - c if flip else c, (y - dy) % NY] if incoming else faces[it].at[c, y]
        return remote(faces[it].at[c, y], slot, face_s.at[it, i], face_r.at[it, i], at(dy, 0, flip))

    def z_copy(it, dz):
        return remote(chosen.at[it, dz], ghost_in.at[it, dz], z_s.at[it, dz], z_r.at[it, dz], at(0, dz, 0))

    def halo_copy(it, up):
        side = 1 if up else 0
        return remote(
            cur.at[0 if up else last], halo.at[it, side], halo_s.at[it, side], halo_r.at[it, side],
            along(NX - 1 if up else 1))

    def matrix_copy(e, to, lower):
        mine, got, ss, rs = (pp.at[last], got_a, a_s, a_r) if lower else (rr.at[0], got_b, b_s, b_r)
        return remote(mine, got.at[e - 1], ss.at[to], rs.at[e - 1], on(to))

    def edge_copy(i):
        dx = JA_STEPS[i]
        return remote(edge_pack.at[ja], edge_pack.at[ja], e_s.at[i], e_r.at[i], along(dx))

    def edge_arrival(i):
        source = (ja - JA_STEPS[i]) % NX
        return remote(edge_pack.at[source], edge_pack.at[source], e_s.at[i], e_r.at[i], along(JA_STEPS[i]))

    def small_copy(it, i, incoming):
        dx = JA_STEPS[i]
        slot = (ja - dx) % NX if incoming else ja
        return remote(small.at[it, ja], small.at[it, slot], g_s.at[it, i], g_r.at[it, i], along(dx))

    def sweep_copy(it, source, to, lower):
        send, got, ss, rs = (sb, bx, x_s, x_r) if lower else (sc, cy, u_s, u_r)
        return remote(send.at[it], got.at[it, source], ss.at[it, to], rs.at[it, source], on(to))

    def residual_bulk(live):
        def step(j, below):
            here = cur[j]
            above = jnp.where(j == last, 0.0, cur[jnp.minimum(j + 1, last)])
            flat = here.reshape(rows, width)

            def shifted(by, axis, size, mask):
                return pltpu.roll(flat, by % size, axis).reshape(vec) * mask[None]

            beside = shifted(1, 1, width, left_ok) + shifted(-1, 1, width, right_ok)
            beside += shifted(1, 0, rows, down_ok) + shifted(-1, 0, rows, up_ok)
            applied = times(diag[j], here) - times(low[j], below) - times(upp[j], above) - COUPLE * beside
            res[j] = live[None] * (forc[j] - applied)
            return here

        lax.fori_loop(0, planes, step, jnp.zeros(vec, F32))

        def start(j, carry):
            sol[j] = times(inv[j], res[j])
            return carry

        lax.fori_loop(1, last, start, 0, unroll=2)

    loads[0].wait()
    loads[1].wait()
    targets = [at(0, d, 0)[0] for d in range(NZ)]

    def find(w, found):
        e = east_ref[w]
        return tuple(jnp.where(e == t, w, f) for t, f in zip(targets, found))

    wests = lax.fori_loop(0, NY * NZ * 2, find, (jnp.int32(0),) * NZ)
    easts = [east_ref[t] for t in targets]
    live = (k_index < depth_ref[zone]).astype(F32)
    ghost_weight = COUPLE * live * edge

    loads[2].wait()

    def mask_plane(j, carry):
        cur[j] = cur[j] * live[None]
        return carry

    lax.fori_loop(0, planes, mask_plane, 0, unroll=2)
    pack_faces(0)
    for i in (3, 4, 5):
        loads[i].wait()

    def premultiply(j, carry):
        for source, target in ((low, mm), (upp, nn)):
            for col in range(nvar):
                target[j, :, col] = OMEGA * times(inv[j], source[j, :, col])
        return carry

    lax.fori_loop(0, planes, premultiply, 0)
    pp[0] = mm[0]
    rr[last] = nn[last]

    def products(s, carry):
        j = last - s
        for col in range(nvar):
            pp[s, :, col] = times(mm[s], pp[s - 1, :, col])
            rr[j, :, col] = times(nn[j], rr[j + 1, :, col])
        return carry

    lax.fori_loop(1, planes, products, 0)
    hh[last] = pp[last]

    def through(s, carry):
        j = last - s
        for col in range(nvar):
            hh[j, :, col] = pp[j, :, col] + times(nn[j], hh[j + 1, :, col])
        return carry

    lax.fori_loop(1, planes, through, 0)
    packets = [jnp.zeros((depth_k, width), F32)] * 3
    for row in range(nvar):
        for col in range(nvar):
            for i, product in enumerate((pp.at[last], rr.at[0], hh.at[0])):
                packets[i] = pack(product[row, col], row * nvar + col, packets[i])
    for i in range(3):
        edge_pack[ja, i] = packets[i]
    loads[6].wait()
    loads[7].wait()
    residual_bulk(live)
    pl.semaphore_wait(barrier, len(partners))

    for it in range(ITERS):
        for i in range(len(FACE_STEPS)):
            face_copy(it, i, False).start()

        @pl.when(ja > 0)
        def _():
            halo_copy(it, True).start()

        @pl.when(ja < NX - 1)
        def _():
            halo_copy(it, False).start()

        if it == 0:
            for i in range(len(JA_STEPS)):
                edge_copy(i).start()
            for lower, pairs in ((True, LOWER_MATS), (False, UPPER_MATS)):
                for e, to in pairs:
                    @pl.when(ja == e)
                    def _(e=e, to=to, lower=lower):
                        matrix_copy(e, to, lower).start()
        else:
            residual_bulk(live)

        @pl.when(ja > 0)
        def _():
            halo_copy(it, False).wait_recv()
            res[0] += live[None] * times(low[0], halo[it, 0])

        @pl.when(ja < NX - 1)
        def _():
            halo_copy(it, True).wait_recv()
            res[last] += live[None] * times(upp[last], halo[it, 1])

        sol[0] = times(inv[0], res[0])
        sol[last] = times(inv[last], res[last])

        def lower_step(j, before):
            value = sol[j] + times(mm[j], before)
            sol[j] = value
            return value

        def upper_step(s, after):
            j = last - s
            value = sol[j] + times(nn[j], after)
            sol[j] = value
            return value

        sb[it] = lax.fori_loop(1, planes, lower_step, sol[0], unroll=True)
        for source, to in LOWER_PAIRS:
            @pl.when(ja == source)
            def _(source=source, to=to):
                sweep_copy(it, source, to, True).start()
        lax.fori_loop(1, planes, upper_step, sol[last], unroll=True)

        for i in range(len(FACE_STEPS)):
            face_copy(it, i, True).wait_recv()
        for dz in Z_STEPS + (0,):
            w, e = wests[dz], easts[dz]
            west = faces[it][w % 2, w // (2 * NZ)]
            east = faces[it][e % 2, e // (2 * NZ)]
            west = jnp.where((w // 2) % NZ == z, west, 0.0)
            east = jnp.where((e // 2) % NZ == z, east, 0.0)
            chosen[it, dz] = jnp.where(odd, pltpu.roll(west, 1, 1), pltpu.roll(east, width - 1, 1))
            if dz:
                z_copy(it, dz).start()

        if it == 0:
            for i in range(len(JA_STEPS)):
                edge_arrival(i).wait_recv()

            def spread(m, carry):
                row, col = m // nvar, m % nvar
                for e in (1, 2, 3):
                    for i in range(3):
                        if e < 3 or i == 2:
                            edge_mat[e, i, row, col] = unpack(edge_pack[e, i], m)
                return carry

            lax.fori_loop(0, nvar * nvar, spread, 0, unroll=5)
            for lower, pairs in ((True, LOWER_MATS), (False, UPPER_MATS)):
                for e, to in pairs:
                    @pl.when(ja == to)
                    def _(e=e, to=to, lower=lower):
                        matrix_copy(e, to, lower).wait_recv()

        for source, to in LOWER_PAIRS:
            @pl.when(ja == to)
            def _(source=source, to=to):
                sweep_copy(it, source, to, True).wait_recv()

        @pl.when(ja == 0)
        def _():
            xin[...] = jnp.zeros(vec, F32)

        @pl.when(ja > 0)
        def _():
            xin[...] = bx[it, 0]

        for e in (1, 2):
            @pl.when(ja > e)
            def _(e=e):
                xin[...] = bx[it, e] + times(got_a[e - 1], xin[...])

        sc[it] = sol[0] + times(hh[0], xin[...])
        for source, to in UPPER_PAIRS:
            @pl.when(ja == source)
            def _(source=source, to=to):
                sweep_copy(it, source, to, False).start()

        for dz in Z_STEPS:
            z_copy(it, dz).wait_recv()
        ghosts = chosen[it, 0]
        for dz in Z_STEPS:
            ghosts += ghost_in[it, dz]
        for m in range(planes * nvar):
            gres[m // nvar, m % nvar] = ghost_weight * unpack(ghosts, m)

        def ghost_start(j, carry):
            mine = gres[j]
            res[j] += mine
            gres[j] = times(inv[j], mine)
            return carry

        lax.fori_loop(0, planes, ghost_start, 0, unroll=4)
        if it == ITERS - 1:
            out_res = pltpu.make_async_copy(res, resid_hbm, out_sem.at[0])
            out_res.start()

        def ghost_lower(j, before):
            value = gres[j] + times(mm[j], before)
            gres[j] = value
            return value

        def ghost_upper(s, after):
            j = last - s
            value = gres[j] + times(nn[j], after)
            sol[j] += value
            return value

        bottom = lax.fori_loop(1, planes, ghost_lower, gres[0], unroll=True)
        sol[last] += bottom
        top = lax.fori_loop(1, planes, ghost_upper, bottom, unroll=True)
        packet = jnp.zeros((depth_k, width), F32)
        for v in range(nvar):
            packet = pack(bottom[v], v, packet)
            packet = pack(top[v], nvar + v, packet)
        small[it, ja] = packet
        for i in range(len(JA_STEPS)):
            small_copy(it, i, False).start()

        for source, to in UPPER_PAIRS:
            @pl.when(ja == to)
            def _(source=source, to=to):
                sweep_copy(it, source, to, False).wait_recv()

        @pl.when(ja == NX - 1)
        def _():
            yin[...] = jnp.zeros(vec, F32)

        @pl.when(ja < NX - 1)
        def _():
            yin[...] = cy[it, NX - 1]

        for e in (2, 1):
            @pl.when(ja < e)
            def _(e=e):
                yin[...] = cy[it, e] + times(got_b[e - 1], yin[...])

        @pl.when(ja > 0)
        def _():
            halo_copy(it, True).wait_send()

        @pl.when(ja < NX - 1)
        def _():
            halo_copy(it, False).wait_send()

        def raise_plane(j, carry):
            cur[j] += sol[j] + times(hh[j], xin[...]) + times(rr[j], yin[...])
            return carry

        lax.fori_loop(0, planes, raise_plane, 0, unroll=2)

        for i in range(len(JA_STEPS)):
            small_copy(it, i, True).wait_recv()
        for e in range(NX):
            for v in range(nvar):
                if e < NX - 1:
                    small_vec[e, v] = edge * unpack(small[it, e], v)
                if e > 0:
                    small_vec[e, nvar + v] = edge * unpack(small[it, e], nvar + v)
        low_end, high_end = pl.ds(0, nvar), pl.ds(nvar, nvar)
        x1 = small_vec[0, low_end]
        x2 = small_vec[1, low_end] + times(edge_mat[1, 0], x1)
        x3 = small_vec[2, low_end] + times(edge_mat[2, 0], x2)
        y2 = small_vec[3, high_end] + times(edge_mat[3, 2], x3)
        y1 = small_vec[2, high_end] + times(edge_mat[2, 2], x2) + times(edge_mat[2, 1], y2)
        y0 = small_vec[1, high_end] + times(edge_mat[1, 2], x1) + times(edge_mat[1, 1], y1)
        xin[...] = jnp.where(ja == 0, 0.0, jnp.where(ja == 1, x1, jnp.where(ja == 2, x2, x3)))
        yin[...] = jnp.where(ja == 3, 0.0, jnp.where(ja == 2, y2, jnp.where(ja == 1, y1, y0)))

        def raise_edges(j, carry):
            cur[j] += times(hh[j], xin[...]) + times(rr[j], yin[...])
            return carry

        lax.fori_loop(0, planes, raise_edges, 0, unroll=4)
        if it < ITERS - 1:
            pack_faces(it + 1)

    out_state = pltpu.make_async_copy(cur, state_hbm, out_sem.at[1])
    out_state.start()
    for it in range(ITERS):
        for i in range(len(FACE_STEPS)):
            face_copy(it, i, False).wait_send()
        for dz in Z_STEPS:
            z_copy(it, dz).wait_send()
        for i in range(len(JA_STEPS)):
            small_copy(it, i, False).wait_send()
        for lower, pairs in ((True, LOWER_PAIRS), (False, UPPER_PAIRS)):
            for source, to in pairs:
                @pl.when(ja == source)
                def _(source=source, to=to, lower=lower):
                    sweep_copy(it, source, to, lower).wait_send()
    for i in range(len(JA_STEPS)):
        edge_copy(i).wait_send()
    for lower, pairs in ((True, LOWER_MATS), (False, UPPER_MATS)):
        for e, to in pairs:
            @pl.when(ja == e)
            def _(e=e, to=to, lower=lower):
                matrix_copy(e, to, lower).wait_send()
    out_res.wait()
    out_state.wait()


def per_device(flow_state, forcing, diag_block, lower_jac, upper_jac, block_inv, east_zone, zone_depth):
    planes, nvar, depth_k, width = flow_state.shape[1:]
    tile = (depth_k, width)
    vec = (nvar,) + tile
    mat = (nvar,) + vec
    dma = pltpu.SemaphoreType.DMA

    def vmem(*shape):
        return pltpu.VMEM(shape, F32)

    ints = pltpu.SMEM(east_zone.shape, jnp.int32)
    state, resid = pl.pallas_call(
        kernel,
        out_shape=[jax.ShapeDtypeStruct((planes,) + vec, F32)] * 2,
        in_specs=[pl.BlockSpec(memory_space=pltpu.HBM)] * 8,
        out_specs=[pl.BlockSpec(memory_space=pltpu.HBM)] * 2,
        scratch_shapes=[ints, ints]
        + [vmem(planes, *vec)] * 2 + [vmem(planes, *mat)] * 4
        + [vmem(planes, *mat)] * 5 + [vmem(planes, *vec)] * 3 + [vmem(2, *mat)] * 2
        + [vmem(NX, 3, *tile), vmem(NX, 3, *mat), vmem(2, NY, *tile), vmem(2, NY, *tile)]
        + [vmem(ITERS, NZ, *tile)] * 2 + [vmem(ITERS, 2, *vec)]
        + [vmem(ITERS, *vec)] * 2 + [vmem(ITERS, NX, *vec)] * 2 + [vmem(*vec)] * 2
        + [vmem(ITERS, NX, *tile), vmem(NX, 2 * nvar, *tile)]
        + [dma((8,)), dma((ITERS, 7)), dma((ITERS, 7)), dma((ITERS, NZ)), dma((ITERS, NZ)), dma((ITERS, 2)), dma((ITERS, 2))]
        + [dma((NX,)), dma((2,)), dma((NX,)), dma((2,)), dma((3,)), dma((3,))]
        + [dma((ITERS, NX))] * 4 + [dma((ITERS, 3))] * 2 + [dma((2,))],
        compiler_params=pltpu.CompilerParams(
            collective_id=0, has_side_effects=True, vmem_limit_bytes=64 * 2**20 - 2**17),
        name="ssor",
    )(east_zone, zone_depth, flow_state[0], forcing[0], diag_block[0], lower_jac[0], upper_jac[0], block_inv[0])
    return state[None], resid[None]


def solution(mesh):
    vec = P("zone", "ja", None, None, None)
    mat = P("zone", "ja", None, None, None, None)
    return jax.shard_map(
        per_device,
        mesh=mesh,
        in_specs=(vec, vec, mat, mat, mat, mat, P(), P()),
        out_specs=(vec, vec),
        check_vma=False,
    )
```

```python
import jax
import jax.numpy as jnp
from jax import lax
from jax.experimental import pallas as pl
from jax.experimental.pallas import tpu as pltpu
from jax.sharding import PartitionSpec as P

ITERS = 2
OMEGA = 1.2
COUPLE = 0.25
NY, NZ, NX = 4, 8, 4
MESH = pl.DeviceIdType.MESH
F32 = jnp.float32
FACE_STEPS = ((2, 1), (2, 0), (1, 1), (3, 1), (1, 0), (3, 0), (0, 1))
Z_STEPS = (4, 3, 5, 2, 6, 1, 7)
JA_STEPS = (2, 1, 3)
LOWER_PAIRS = ((0, 2, 0), (1, 3, 0), (1, 2, 0), (2, 3, 0), (0, 1, 0), (0, 3, 1))
UPPER_PAIRS = ((3, 1, 0), (2, 0, 0), (3, 0, 0), (3, 2, 0), (2, 1, 0), (1, 0, 0))
LOWER_MATS = ((1, 0), (1, 2), (2, 3))
UPPER_MATS = ((2, 1), (1, 0), (2, 0))


def kernel(
    east_hbm, depth_hbm, flow_hbm, forc_hbm, diag_hbm, low_hbm, upp_hbm, inv_hbm,
    cur, res,
    east_ref, depth_ref, forc, diag, low, upp, inv,
    mm, nn, pp, rr, hh, gres, sol, got_a, got_b,
    edge_pack, edge_mat, face0, face1, chosen, ghost_in, halo,
    sb, sc, bx, cy, xin, yin, small, small_vec,
    load_sem, face_s, face_r, z_s, z_r, halo_s, halo_r,
    a_s, a_r, b_s, b_r, e_s, e_r, x_s, x_r, u_s, u_r, g_s, g_r,
):
    planes, nvar, depth_k, width = cur.shape
    rows = nvar * depth_k
    last = planes - 1
    vec = (nvar, depth_k, width)
    faces = (face0, face1)
    zone = lax.axis_index("zone")
    ja = lax.axis_index("ja")
    y, z, c = zone // (2 * NZ), (zone // 2) % NZ, zone % 2

    def at(dy, dz, flip):
        core = 1 - c if flip else c
        return (((y + dy) % NY) * (2 * NZ) + ((z + dz) % NZ) * 2 + core, ja)

    def along(dx):
        return (zone, (ja + dx) % NX)

    def on(device):
        return (zone, jnp.int32(device))

    barrier = pltpu.get_barrier_semaphore()
    partners = [at(dy, 0, flip) for dy, flip in FACE_STEPS] + [at(0, d, 0) for d in Z_STEPS]
    partners += [along(d) for d in JA_STEPS]
    for partner in partners:
        pl.semaphore_signal(barrier, 1, device_id=partner, device_id_type=MESH)

    sources = (
        (east_hbm, east_ref), (depth_hbm, depth_ref), (flow_hbm, cur), (inv_hbm, inv),
        (low_hbm, low), (upp_hbm, upp), (diag_hbm, diag), (forc_hbm, forc))
    loads = [pltpu.make_async_copy(src, dst, load_sem.at[i]) for i, (src, dst) in enumerate(sources)]
    for load in loads:
        load.start()

    k_index = lax.broadcasted_iota(jnp.int32, (depth_k, width), 0)
    lane = lax.broadcasted_iota(jnp.int32, (depth_k, width), 1)
    edge = ((lane == 0) | (lane == width - 1)).astype(F32)
    left_ok = (lane > 0).astype(F32)
    right_ok = (lane < width - 1).astype(F32)
    down_ok = (k_index > 0).astype(F32)
    up_ok = (k_index < depth_k - 1).astype(F32)
    odd = lane % 2 == 1

    def remote(src, dst, ss, rs, device):
        return pltpu.make_async_remote_copy(src, dst, ss, rs, device_id=device, device_id_type=MESH)

    def times(mat, v):
        out = mat[:, 0] * v[0][None]
        for col in range(1, nvar):
            out += mat[:, col] * v[col][None]
        return out

    def pack(tile, m, packet):
        turned = pltpu.roll(tile, 2 * m + 1, 1)
        return jnp.where((lane == 2 * m) | (lane == 2 * m + 1), turned, packet)

    def unpack(packet, m):
        return pltpu.roll(packet, width - 1 - 2 * m, 1)

    def pack_faces(it):
        packet = jnp.zeros((depth_k, width), F32)
        for m in range(planes * nvar):
            packet = pack(cur[m // nvar, m % nvar], m, packet)
        faces[it][c, y] = packet

    def face_copy(it, i, incoming):
        dy, flip = FACE_STEPS[i]
        slot = faces[it].at[1 - c if flip else c, (y - dy) % NY] if incoming else faces[it].at[c, y]
        return remote(faces[it].at[c, y], slot, face_s.at[it, i], face_r.at[it, i], at(dy, 0, flip))

    def z_copy(it, dz):
        return remote(chosen.at[it, dz], ghost_in.at[it, dz], z_s.at[it, dz], z_r.at[it, dz], at(0, dz, 0))

    def halo_copy(it, up):
        side = 1 if up else 0
        return remote(
            cur.at[0 if up else last], halo.at[it, side], halo_s.at[it, side], halo_r.at[it, side],
            along(NX - 1 if up else 1))

    def matrix_copy(e, to, lower):
        if lower:
            return remote(pp.at[last], got_a, a_s.at[to // 2], a_r, on(to))
        return remote(rr.at[0], got_b.at[e - 1], b_s.at[to], b_r.at[e - 1], on(to))

    def edge_copy(i):
        dx = JA_STEPS[i]
        return remote(edge_pack.at[ja], edge_pack.at[ja], e_s.at[i], e_r.at[i], along(dx))

    def edge_arrival(i):
        source = (ja - JA_STEPS[i]) % NX
        return remote(edge_pack.at[source], edge_pack.at[source], e_s.at[i], e_r.at[i], along(JA_STEPS[i]))

    def small_copy(it, i, incoming):
        dx = JA_STEPS[i]
        slot = (ja - dx) % NX if incoming else ja
        return remote(small.at[it, ja], small.at[it, slot], g_s.at[it, i], g_r.at[it, i], along(dx))

    def sweep_copy(it, source, to, through, lower):
        send = sb.at[it, through] if lower else sc.at[it]
        got, ss, rs = (bx, x_s, x_r) if lower else (cy, u_s, u_r)
        return remote(send, got.at[it, source], ss.at[it, to], rs.at[it, source], on(to))

    def send_matrices(lower):
        for e, to in LOWER_MATS if lower else UPPER_MATS:
            @pl.when(ja == e)
            def _(e=e, to=to):
                matrix_copy(e, to, lower).start()

    def await_matrices(device, lower):
        for e, to in LOWER_MATS if lower else UPPER_MATS:
            if to == device:
                @pl.when(ja == device)
                def _(e=e):
                    matrix_copy(e, device, lower).wait_recv()

    def send_sweep(it, through, lower):
        for source, to, kind in LOWER_PAIRS if lower else UPPER_PAIRS:
            if kind == through:
                @pl.when(ja == source)
                def _(source=source, to=to):
                    sweep_copy(it, source, to, through, lower).start()

    def await_sweep(it, lower):
        for source, to, kind in LOWER_PAIRS if lower else UPPER_PAIRS:
            @pl.when(ja == to)
            def _(source=source, to=to, kind=kind):
                sweep_copy(it, source, to, kind, lower).wait_recv()

    def residual_bulk(live):
        def step(j, below):
            here = cur[j]
            above = jnp.where(j == last, 0.0, cur[jnp.minimum(j + 1, last)])
            flat = here.reshape(rows, width)

            def shifted(by, axis, size, mask):
                return pltpu.roll(flat, by % size, axis).reshape(vec) * mask[None]

            beside = shifted(1, 1, width, left_ok) + shifted(-1, 1, width, right_ok)
            beside += shifted(1, 0, rows, down_ok) + shifted(-1, 0, rows, up_ok)
            applied = times(diag[j], here) - times(low[j], below) - times(upp[j], above) - COUPLE * beside
            res[j] = live[None] * (forc[j] - applied)
            return here

        lax.fori_loop(0, planes, step, jnp.zeros(vec, F32))

        def start(j, carry):
            sol[j] = times(inv[j], res[j])
            return carry

        lax.fori_loop(1, last, start, 0, unroll=2)

    loads[0].wait()
    loads[1].wait()
    targets = [at(0, d, 0)[0] for d in range(NZ)]

    def find(w, found):
        e = east_ref[w]
        return tuple(jnp.where(e == t, w, f) for t, f in zip(targets, found))

    wests = lax.fori_loop(0, NY * NZ * 2, find, (jnp.int32(0),) * NZ)
    easts = [east_ref[t] for t in targets]
    live = (k_index < depth_ref[zone]).astype(F32)
    ghost_weight = COUPLE * live * edge

    loads[2].wait()

    def mask_plane(j, carry):
        cur[j] = cur[j] * live[None]
        return carry

    lax.fori_loop(0, planes, mask_plane, 0, unroll=2)
    pack_faces(0)
    for i in (3, 4, 5):
        loads[i].wait()

    def premultiply(j, carry):
        for source, target in ((low, mm), (upp, nn)):
            for col in range(nvar):
                target[j, :, col] = OMEGA * times(inv[j], source[j, :, col])
        return carry

    lax.fori_loop(0, planes, premultiply, 0)
    pp[0] = mm[0]
    rr[last] = nn[last]

    def products(s, carry):
        j = last - s
        for col in range(nvar):
            pp[s, :, col] = times(mm[s], pp[s - 1, :, col])
            rr[j, :, col] = times(nn[j], rr[j + 1, :, col])
        return carry

    lax.fori_loop(1, planes, products, 0)
    hh[last] = pp[last]

    def through(s, carry):
        j = last - s
        for col in range(nvar):
            hh[j, :, col] = pp[j, :, col] + times(nn[j], hh[j + 1, :, col])
        return carry

    lax.fori_loop(1, planes, through, 0)
    packets = [jnp.zeros((depth_k, width), F32)] * 3
    for row in range(nvar):
        for col in range(nvar):
            for i, product in enumerate((pp.at[last], rr.at[0], hh.at[0])):
                packets[i] = pack(product[row, col], row * nvar + col, packets[i])
    for i in range(3):
        edge_pack[ja, i] = packets[i]
    loads[6].wait()
    loads[7].wait()
    residual_bulk(live)
    pl.semaphore_wait(barrier, len(partners))

    for it in range(ITERS):
        for i in range(len(FACE_STEPS)):
            face_copy(it, i, False).start()

        @pl.when(ja > 0)
        def _():
            halo_copy(it, True).start()

        @pl.when(ja < NX - 1)
        def _():
            halo_copy(it, False).start()

        if it == 0:
            send_matrices(True)
        else:
            residual_bulk(live)

        @pl.when(ja > 0)
        def _():
            halo_copy(it, False).wait_recv()
            res[0] += live[None] * times(low[0], halo[it, 0])

        @pl.when(ja < NX - 1)
        def _():
            halo_copy(it, True).wait_recv()
            res[last] += live[None] * times(upp[last], halo[it, 1])

        sol[0] = times(inv[0], res[0])
        sol[last] = times(inv[last], res[last])

        def through_lower(it):
            @pl.when(ja == 0)
            def _():
                sb[it, 1] = times(got_a, sb[it, 0])

            send_sweep(it, 1, True)

        def lower_step(j, before):
            value = sol[j] + times(mm[j], before)
            sol[j] = value
            return value

        def upper_step(s, after):
            j = last - s
            value = sol[j] + times(nn[j], after)
            sol[j] = value
            return value

        sb[it, 0] = lax.fori_loop(1, planes, lower_step, sol[0], unroll=True)
        send_sweep(it, 0, True)
        if it == 0:
            send_matrices(False)
            @pl.when(ja > 0)
            def _():
                for i in range(len(JA_STEPS)):
                    edge_copy(i).start()
        else:
            through_lower(it)
        sc[it] = lax.fori_loop(1, planes, upper_step, sol[last], unroll=True)

        for i in range(len(FACE_STEPS)):
            face_copy(it, i, True).wait_recv()
        for dz in Z_STEPS + (0,):
            w, e = wests[dz], easts[dz]
            west = faces[it][w % 2, w // (2 * NZ)]
            east = faces[it][e % 2, e // (2 * NZ)]
            west = jnp.where((w // 2) % NZ == z, west, 0.0)
            east = jnp.where((e // 2) % NZ == z, east, 0.0)
            chosen[it, dz] = jnp.where(odd, pltpu.roll(west, 1, 1), pltpu.roll(east, width - 1, 1))
            if dz:
                z_copy(it, dz).start()

        def lower_inflow():
            await_sweep(it, True)

            @pl.when(ja == 0)
            def _():
                xin[...] = jnp.zeros(vec, F32)

            @pl.when(ja == 1)
            def _():
                xin[...] = bx[it, 0]

            @pl.when(ja == 2)
            def _():
                xin[...] = bx[it, 1] + times(got_a, bx[it, 0])

            @pl.when(ja == 3)
            def _():
                xin[...] = bx[it, 2] + times(got_a, bx[it, 1] + bx[it, 0])

            sc[it] += times(hh[0], xin[...])
            send_sweep(it, 0, False)


        def ghost_response():
            for dz in Z_STEPS:
                z_copy(it, dz).wait_recv()
            ghosts = chosen[it, 0]
            for dz in Z_STEPS:
                ghosts += ghost_in[it, dz]
            for m in range(planes * nvar):
                gres[m // nvar, m % nvar] = ghost_weight * unpack(ghosts, m)

            def ghost_start(j, carry):
                mine = gres[j]
                res[j] += mine
                gres[j] = times(inv[j], mine)
                return carry

            lax.fori_loop(0, planes, ghost_start, 0, unroll=4)

            def ghost_lower(j, before):
                value = gres[j] + times(mm[j], before)
                gres[j] = value
                return value

            def ghost_upper(s, after):
                j = last - s
                value = gres[j] + times(nn[j], after)
                sol[j] += value
                return value

            bottom = lax.fori_loop(1, planes, ghost_lower, gres[0], unroll=True)
            sol[last] += bottom
            top = lax.fori_loop(1, planes, ghost_upper, bottom, unroll=True)
            packet = jnp.zeros((depth_k, width), F32)
            for v in range(nvar):
                packet = pack(bottom[v], v, packet)
                packet = pack(top[v], nvar + v, packet)
            small[it, ja] = packet
            for i in range(len(JA_STEPS)):
                small_copy(it, i, False).start()


        if it == 0:
            await_matrices(0, True)
            through_lower(it)
            await_matrices(2, True)
            pl.when(ja < NX - 1)(lower_inflow)
            ghost_response()
            await_matrices(NX - 1, True)
            pl.when(ja == NX - 1)(lower_inflow)
        else:
            lower_inflow()
            ghost_response()

        if it == 0:
            for i in range(len(JA_STEPS)):
                pl.when(ja != JA_STEPS[i])(edge_arrival(i).wait_recv)

            def spread(m, carry):
                row, col = m // nvar, m % nvar
                for e in (1, 2, 3):
                    for i in range(3):
                        if e < 3 or i == 2:
                            edge_mat[e, i, row, col] = unpack(edge_pack[e, i], m)
                return carry

            lax.fori_loop(0, nvar * nvar, spread, 0, unroll=5)
        if it == 0:
            await_matrices(1, False)
            await_matrices(0, False)
        await_sweep(it, False)

        @pl.when(ja == 3)
        def _():
            yin[...] = jnp.zeros(vec, F32)

        @pl.when(ja == 2)
        def _():
            yin[...] = cy[it, 3]

        @pl.when(ja == 1)
        def _():
            yin[...] = cy[it, 2] + times(got_b[1], cy[it, 3])

        @pl.when(ja == 0)
        def _():
            yin[...] = cy[it, 1] + times(got_b[0], cy[it, 2] + times(got_b[1], cy[it, 3]))

        @pl.when(ja > 0)
        def _():
            halo_copy(it, True).wait_send()

        @pl.when(ja < NX - 1)
        def _():
            halo_copy(it, False).wait_send()

        def raise_plane(j, carry):
            cur[j] += sol[j] + times(hh[j], xin[...]) + times(rr[j], yin[...])
            return carry

        lax.fori_loop(0, planes, raise_plane, 0, unroll=2)

        for i in range(len(JA_STEPS)):
            small_copy(it, i, True).wait_recv()
        for e in range(NX):
            for v in range(nvar):
                if e < NX - 1:
                    small_vec[e, v] = edge * unpack(small[it, e], v)
                if e > 0:
                    small_vec[e, nvar + v] = edge * unpack(small[it, e], nvar + v)
        low_end, high_end = pl.ds(0, nvar), pl.ds(nvar, nvar)
        x1 = small_vec[0, low_end]
        x2 = small_vec[1, low_end] + times(edge_mat[1, 0], x1)
        x3 = small_vec[2, low_end] + times(edge_mat[2, 0], x2)
        y2 = small_vec[3, high_end] + times(edge_mat[3, 2], x3)
        y1 = small_vec[2, high_end] + times(edge_mat[2, 2], x2) + times(edge_mat[2, 1], y2)
        y0 = small_vec[1, high_end] + times(edge_mat[1, 2], x1) + times(edge_mat[1, 1], y1)
        xin[...] = jnp.where(ja == 0, 0.0, jnp.where(ja == 1, x1, jnp.where(ja == 2, x2, x3)))
        yin[...] = jnp.where(ja == 3, 0.0, jnp.where(ja == 2, y2, jnp.where(ja == 1, y1, y0)))

        def raise_edges(j, carry):
            cur[j] += times(hh[j], xin[...]) + times(rr[j], yin[...])
            return carry

        lax.fori_loop(0, planes, raise_edges, 0, unroll=4)
        if it < ITERS - 1:
            pack_faces(it + 1)

    for it in range(ITERS):
        for i in range(len(FACE_STEPS)):
            face_copy(it, i, False).wait_send()
        for dz in Z_STEPS:
            z_copy(it, dz).wait_send()
        for i in range(len(JA_STEPS)):
            small_copy(it, i, False).wait_send()
        for lower, pairs in ((True, LOWER_PAIRS), (False, UPPER_PAIRS)):
            for source, to, kind in pairs:
                @pl.when(ja == source)
                def _(source=source, to=to, kind=kind, lower=lower):
                    sweep_copy(it, source, to, kind, lower).wait_send()

    @pl.when(ja > 0)
    def _():
        for i in range(len(JA_STEPS)):
            edge_copy(i).wait_send()

    for lower, pairs in ((True, LOWER_MATS), (False, UPPER_MATS)):
        for e, to in pairs:
            @pl.when(ja == e)
            def _(e=e, to=to, lower=lower):
                matrix_copy(e, to, lower).wait_send()


def write_out(state_ref, resid_ref, state_out, resid_out, sems):
    copies = [
        pltpu.make_async_copy(state_ref, state_out, sems.at[0]),
        pltpu.make_async_copy(resid_ref, resid_out, sems.at[1]),
    ]
    for copy in copies:
        copy.start()
    for copy in copies:
        copy.wait()


def per_device(flow_state, forcing, diag_block, lower_jac, upper_jac, block_inv, east_zone, zone_depth):
    planes, nvar, depth_k, width = flow_state.shape[1:]
    tile = (depth_k, width)
    vec = (nvar,) + tile
    mat = (nvar,) + vec
    dma = pltpu.SemaphoreType.DMA

    def vmem(*shape):
        return pltpu.VMEM(shape, F32)

    ints = pltpu.SMEM(east_zone.shape, jnp.int32)
    state, resid = pl.pallas_call(
        kernel,
        out_shape=[pltpu.VMEM((planes,) + vec, F32)] * 2,
        in_specs=[pl.BlockSpec(memory_space=pltpu.HBM)] * 8,
        out_specs=[pl.BlockSpec(memory_space=pltpu.VMEM)] * 2,
        scratch_shapes=[ints, ints]
        + [vmem(planes, *vec)] + [vmem(planes, *mat)] * 4
        + [vmem(planes, *mat)] * 5 + [vmem(planes, *vec)] * 2 + [vmem(*mat), vmem(2, *mat)]
        + [vmem(NX, 3, *tile), vmem(NX, 3, *mat), vmem(2, NY, *tile), vmem(2, NY, *tile)]
        + [vmem(ITERS, NZ, *tile)] * 2 + [vmem(ITERS, 2, *vec)]
        + [vmem(ITERS, 2, *vec), vmem(ITERS, *vec)] + [vmem(ITERS, NX, *vec)] * 2 + [vmem(*vec)] * 2
        + [vmem(ITERS, NX, *tile), vmem(NX, 2 * nvar, *tile)]
        + [dma((8,)), dma((ITERS, 7)), dma((ITERS, 7)), dma((ITERS, NZ)), dma((ITERS, NZ)), dma((ITERS, 2)), dma((ITERS, 2))]
        + [dma((2,)), dma, dma((2,)), dma((2,)), dma((3,)), dma((3,))]
        + [dma((ITERS, NX))] * 4 + [dma((ITERS, 3))] * 2,
        compiler_params=pltpu.CompilerParams(
            collective_id=0, has_side_effects=True, vmem_limit_bytes=63 * 2**20),
        name="ssor",
    )(east_zone, zone_depth, flow_state[0], forcing[0], diag_block[0], lower_jac[0], upper_jac[0], block_inv[0])
    state, resid = pl.pallas_call(
        write_out,
        out_shape=[jax.ShapeDtypeStruct((planes,) + vec, F32)] * 2,
        in_specs=[pl.BlockSpec(memory_space=pltpu.VMEM)] * 2,
        out_specs=[pl.BlockSpec(memory_space=pltpu.HBM)] * 2,
        scratch_shapes=[dma((2,))],
        name="write_out",
    )(*(pltpu.with_memory_space_constraint(array, pltpu.VMEM) for array in (state, resid)))
    return state[None], resid[None]


def solution(mesh):
    vec = P("zone", "ja", None, None, None)
    mat = P("zone", "ja", None, None, None, None)
    return jax.shard_map(
        per_device,
        mesh=mesh,
        in_specs=(vec, vec, mat, mat, mat, mat, P(), P()),
        out_specs=(vec, vec),
        check_vma=False,
    )
```

```python
import jax
import jax.numpy as jnp
from jax import lax
from jax.experimental import pallas as pl
from jax.experimental.pallas import tpu as pltpu
from jax.sharding import PartitionSpec as P

ITERS = 2
OMEGA = 1.2
COUPLE = 0.25
NY, NZ, NX = 4, 8, 4
MESH = pl.DeviceIdType.MESH
F32 = jnp.float32
FACE_STEPS = ((2, 1), (2, 0), (1, 1), (3, 1), (1, 0), (3, 0), (0, 1))
Z_STEPS = (4, 3, 5, 2, 6, 1, 7)
JA_STEPS = (2, 1, 3)
LOWER_PAIRS = ((0, 2, 0), (1, 3, 0), (1, 2, 0), (2, 3, 0), (0, 1, 0), (0, 3, 1))
UPPER_PAIRS = ((3, 1, 0), (2, 0, 0), (3, 0, 0), (3, 2, 0), (2, 1, 0), (1, 0, 0))
LOWER_MATS = ((1, 0), (1, 2), (2, 3))
UPPER_MATS = ((2, 1), (1, 0), (2, 0))


def kernel(
    east_hbm, depth_hbm, flow_hbm, forc_hbm, diag_hbm, low_hbm, upp_hbm, inv_hbm,
    cur, res,
    east_ref, depth_ref, forc, diag, low, upp, inv,
    mm, nn, pp, rr, hh, gres, sol, got_a, got_b,
    edge_pack, edge_mat, face0, face1, chosen, ghost_in, halo,
    sb, sc, bx, cy, xin, yin, ghost_x, ghost_y, small, small_vec,
    load_sem, face_s, face_r, z_s, z_r, halo_s, halo_r,
    a_s, a_r, b_s, b_r, e_s, e_r, x_s, x_r, u_s, u_r, g_s, g_r,
):
    planes, nvar, depth_k, width = cur.shape
    rows = nvar * depth_k
    last = planes - 1
    vec = (nvar, depth_k, width)
    faces = (face0, face1)
    zone = lax.axis_index("zone")
    ja = lax.axis_index("ja")
    y, z, c = zone // (2 * NZ), (zone // 2) % NZ, zone % 2

    def at(dy, dz, flip):
        core = 1 - c if flip else c
        return (((y + dy) % NY) * (2 * NZ) + ((z + dz) % NZ) * 2 + core, ja)

    def along(dx):
        return (zone, (ja + dx) % NX)

    def on(device):
        return (zone, jnp.int32(device))

    barrier = pltpu.get_barrier_semaphore()
    partners = [at(dy, 0, flip) for dy, flip in FACE_STEPS] + [at(0, d, 0) for d in Z_STEPS]
    partners += [along(d) for d in JA_STEPS]
    for partner in partners:
        pl.semaphore_signal(barrier, 1, device_id=partner, device_id_type=MESH)

    sources = (
        (east_hbm, east_ref), (depth_hbm, depth_ref), (flow_hbm, cur), (inv_hbm, inv),
        (low_hbm, low), (upp_hbm, upp), (diag_hbm, diag), (forc_hbm, forc))
    loads = [pltpu.make_async_copy(src, dst, load_sem.at[i]) for i, (src, dst) in enumerate(sources)]
    for load in loads:
        load.start()

    k_index = lax.broadcasted_iota(jnp.int32, (depth_k, width), 0)
    lane = lax.broadcasted_iota(jnp.int32, (depth_k, width), 1)
    edge = ((lane == 0) | (lane == width - 1)).astype(F32)
    left_ok = (lane > 0).astype(F32)
    right_ok = (lane < width - 1).astype(F32)
    down_ok = (k_index > 0).astype(F32)
    up_ok = (k_index < depth_k - 1).astype(F32)
    odd = lane % 2 == 1

    def remote(src, dst, ss, rs, device):
        return pltpu.make_async_remote_copy(src, dst, ss, rs, device_id=device, device_id_type=MESH)

    def times(mat, v):
        out = mat[:, 0] * v[0][None]
        for col in range(1, nvar):
            out += mat[:, col] * v[col][None]
        return out

    def pack(tile, m, packet):
        turned = pltpu.roll(tile, 2 * m + 1, 1)
        return jnp.where((lane == 2 * m) | (lane == 2 * m + 1), turned, packet)

    def unpack(packet, m):
        return pltpu.roll(packet, width - 1 - 2 * m, 1)

    def pack_faces(it):
        packet = jnp.zeros((depth_k, width), F32)
        for m in range(planes * nvar):
            packet = pack(cur[m // nvar, m % nvar], m, packet)
        faces[it][c, y] = packet

    def face_copy(it, i, incoming):
        dy, flip = FACE_STEPS[i]
        slot = faces[it].at[1 - c if flip else c, (y - dy) % NY] if incoming else faces[it].at[c, y]
        return remote(faces[it].at[c, y], slot, face_s.at[it, i], face_r.at[it, i], at(dy, 0, flip))

    def z_copy(it, dz):
        return remote(chosen.at[it, dz], ghost_in.at[it, dz], z_s.at[it, dz], z_r.at[it, dz], at(0, dz, 0))

    def halo_copy(it, up):
        side = 1 if up else 0
        return remote(
            cur.at[0 if up else last], halo.at[it, side], halo_s.at[it, side], halo_r.at[it, side],
            along(NX - 1 if up else 1))

    def matrix_copy(e, to, lower):
        if lower:
            return remote(pp.at[last], got_a, a_s.at[to // 2], a_r, on(to))
        return remote(rr.at[0], got_b.at[e - 1], b_s.at[to], b_r.at[e - 1], on(to))

    def edge_copy(i):
        dx = JA_STEPS[i]
        return remote(edge_pack.at[ja], edge_pack.at[ja], e_s.at[i], e_r.at[i], along(dx))

    def edge_arrival(i):
        source = (ja - JA_STEPS[i]) % NX
        return remote(edge_pack.at[source], edge_pack.at[source], e_s.at[i], e_r.at[i], along(JA_STEPS[i]))

    def small_copy(it, i, incoming):
        dx = JA_STEPS[i]
        slot = (ja - dx) % NX if incoming else ja
        return remote(small.at[it, ja], small.at[it, slot], g_s.at[it, i], g_r.at[it, i], along(dx))

    def sweep_copy(it, source, to, through, lower):
        send = sb.at[it, through] if lower else sc.at[it]
        got, ss, rs = (bx, x_s, x_r) if lower else (cy, u_s, u_r)
        return remote(send, got.at[it, source], ss.at[it, to], rs.at[it, source], on(to))

    def send_matrices(lower):
        for e, to in LOWER_MATS if lower else UPPER_MATS:
            @pl.when(ja == e)
            def _(e=e, to=to):
                matrix_copy(e, to, lower).start()

    def await_matrices(device, lower):
        for e, to in LOWER_MATS if lower else UPPER_MATS:
            if to == device:
                @pl.when(ja == device)
                def _(e=e):
                    matrix_copy(e, device, lower).wait_recv()

    def send_sweep(it, through, lower):
        for source, to, kind in LOWER_PAIRS if lower else UPPER_PAIRS:
            if kind == through:
                @pl.when(ja == source)
                def _(source=source, to=to):
                    sweep_copy(it, source, to, through, lower).start()

    def await_sweep(it, lower):
        for source, to, kind in LOWER_PAIRS if lower else UPPER_PAIRS:
            @pl.when(ja == to)
            def _(source=source, to=to, kind=kind):
                sweep_copy(it, source, to, kind, lower).wait_recv()

    def residual_bulk(live):
        def step(j, below):
            here = cur[j]
            above = jnp.where(j == last, 0.0, cur[jnp.minimum(j + 1, last)])
            flat = here.reshape(rows, width)

            def shifted(by, axis, size, mask):
                return pltpu.roll(flat, by % size, axis).reshape(vec) * mask[None]

            beside = shifted(1, 1, width, left_ok) + shifted(-1, 1, width, right_ok)
            beside += shifted(1, 0, rows, down_ok) + shifted(-1, 0, rows, up_ok)
            applied = times(diag[j], here) - times(low[j], below) - times(upp[j], above) - COUPLE * beside
            res[j] = live[None] * (forc[j] - applied)
            return here

        lax.fori_loop(0, planes, step, jnp.zeros(vec, F32))

        def start(j, carry):
            sol[j] = times(inv[j], res[j])
            return carry

        lax.fori_loop(1, last, start, 0, unroll=2)

    loads[0].wait()
    loads[1].wait()
    targets = [at(0, d, 0)[0] for d in range(NZ)]

    def find(w, found):
        e = east_ref[w]
        return tuple(jnp.where(e == t, w, f) for t, f in zip(targets, found))

    wests = lax.fori_loop(0, NY * NZ * 2, find, (jnp.int32(0),) * NZ)
    easts = [east_ref[t] for t in targets]
    live = (k_index < depth_ref[zone]).astype(F32)
    ghost_weight = COUPLE * live * edge

    loads[2].wait()

    def mask_plane(j, carry):
        cur[j] = cur[j] * live[None]
        return carry

    lax.fori_loop(0, planes, mask_plane, 0, unroll=2)
    pack_faces(0)
    for i in (3, 4, 5):
        loads[i].wait()

    def premultiply(j, carry):
        for source, target in ((low, mm), (upp, nn)):
            for col in range(nvar):
                target[j, :, col] = OMEGA * times(inv[j], source[j, :, col])
        return carry

    lax.fori_loop(0, planes, premultiply, 0)
    pp[0] = mm[0]
    rr[last] = nn[last]

    def products(s, carry):
        j = last - s
        for col in range(nvar):
            pp[s, :, col] = times(mm[s], pp[s - 1, :, col])
            rr[j, :, col] = times(nn[j], rr[j + 1, :, col])
        return carry

    lax.fori_loop(1, planes, products, 0)
    hh[last] = pp[last]

    def through(s, carry):
        j = last - s
        for col in range(nvar):
            hh[j, :, col] = pp[j, :, col] + times(nn[j], hh[j + 1, :, col])
        return carry

    lax.fori_loop(1, planes, through, 0)
    packets = [jnp.zeros((depth_k, width), F32)] * 2
    for row in range(nvar):
        for col in range(nvar):
            m = row * nvar + col
            packets[0] = pack(pp[last, row, col], m, packets[0])
            packets[0] = pack(rr[0, row, col], nvar * nvar + m, packets[0])
            packets[1] = pack(hh[0, row, col], m, packets[1])
    for i in range(2):
        edge_pack[ja, i] = packets[i]
    loads[6].wait()
    loads[7].wait()
    residual_bulk(live)
    pl.semaphore_wait(barrier, len(partners))

    for it in range(ITERS):
        for i in range(len(FACE_STEPS)):
            face_copy(it, i, False).start()

        @pl.when(ja > 0)
        def _():
            halo_copy(it, True).start()

        @pl.when(ja < NX - 1)
        def _():
            halo_copy(it, False).start()

        if it == 0:
            send_matrices(True)
        else:
            residual_bulk(live)

        @pl.when(ja > 0)
        def _():
            halo_copy(it, False).wait_recv()
            res[0] += live[None] * times(low[0], halo[it, 0])

        @pl.when(ja < NX - 1)
        def _():
            halo_copy(it, True).wait_recv()
            res[last] += live[None] * times(upp[last], halo[it, 1])

        sol[0] = times(inv[0], res[0])
        sol[last] = times(inv[last], res[last])

        def through_lower(it):
            @pl.when(ja == 0)
            def _():
                sb[it, 1] = times(got_a, sb[it, 0])

            send_sweep(it, 1, True)

        def lower_step(j, before):
            value = sol[j] + times(mm[j], before)
            sol[j] = value
            return value

        def upper_step(s, after):
            j = last - s
            value = sol[j] + times(nn[j], after)
            sol[j] = value
            return value

        sb[it, 0] = lax.fori_loop(1, planes, lower_step, sol[0], unroll=True)
        send_sweep(it, 0, True)
        if it == 0:
            send_matrices(False)
            @pl.when(ja > 0)
            def _():
                for i in range(len(JA_STEPS)):
                    edge_copy(i).start()
        else:
            through_lower(it)
        sc[it] = lax.fori_loop(1, planes, upper_step, sol[last], unroll=True)

        for i in range(len(FACE_STEPS)):
            face_copy(it, i, True).wait_recv()
        for dz in Z_STEPS + (0,):
            w, e = wests[dz], easts[dz]
            west = faces[it][w % 2, w // (2 * NZ)]
            east = faces[it][e % 2, e // (2 * NZ)]
            west = jnp.where((w // 2) % NZ == z, west, 0.0)
            east = jnp.where((e // 2) % NZ == z, east, 0.0)
            chosen[it, dz] = jnp.where(odd, pltpu.roll(west, 1, 1), pltpu.roll(east, width - 1, 1))
            if dz:
                z_copy(it, dz).start()

        def lower_inflow():
            await_sweep(it, True)

            @pl.when(ja == 0)
            def _():
                xin[...] = jnp.zeros(vec, F32)

            @pl.when(ja == 1)
            def _():
                xin[...] = bx[it, 0]

            @pl.when(ja == 2)
            def _():
                xin[...] = bx[it, 1] + times(got_a, bx[it, 0])

            @pl.when(ja == 3)
            def _():
                xin[...] = bx[it, 2] + times(got_a, bx[it, 1] + bx[it, 0])

            sc[it] += times(hh[0], xin[...])
            send_sweep(it, 0, False)


        def ghost_response():
            for dz in Z_STEPS:
                z_copy(it, dz).wait_recv()
            ghosts = chosen[it, 0]
            for dz in Z_STEPS:
                ghosts += ghost_in[it, dz]
            for m in range(planes * nvar):
                gres[m // nvar, m % nvar] = ghost_weight * unpack(ghosts, m)

            def ghost_start(j, carry):
                mine = gres[j]
                res[j] += mine
                gres[j] = times(inv[j], mine)
                return carry

            lax.fori_loop(0, planes, ghost_start, 0, unroll=4)

            def ghost_lower(j, before):
                value = gres[j] + times(mm[j], before)
                gres[j] = value
                return value

            def ghost_upper(s, after):
                j = last - s
                value = gres[j] + times(nn[j], after)
                sol[j] += value
                return value

            bottom = lax.fori_loop(1, planes, ghost_lower, gres[0], unroll=True)
            sol[last] += bottom
            top = lax.fori_loop(1, planes, ghost_upper, bottom, unroll=True)
            packet = jnp.zeros((depth_k, width), F32)
            for v in range(nvar):
                packet = pack(bottom[v], v, packet)
                packet = pack(top[v], nvar + v, packet)
            small[it, ja] = packet
            for i in range(len(JA_STEPS)):
                small_copy(it, i, False).start()


        if it == 0:
            await_matrices(0, True)
            through_lower(it)
            await_matrices(2, True)
            pl.when(ja < NX - 1)(lower_inflow)
            ghost_response()
            await_matrices(NX - 1, True)
            pl.when(ja == NX - 1)(lower_inflow)
        else:
            lower_inflow()
            ghost_response()

        if it == 0:
            for i in range(len(JA_STEPS)):
                pl.when(ja != JA_STEPS[i])(edge_arrival(i).wait_recv)

            def spread(m, carry):
                row, col = m // nvar, m % nvar
                for e in (1, 2, 3):
                    edge_mat[e, 2, row, col] = unpack(edge_pack[e, 1], m)
                    if e < 3:
                        edge_mat[e, 0, row, col] = unpack(edge_pack[e, 0], m)
                        edge_mat[e, 1, row, col] = unpack(edge_pack[e, 0], nvar * nvar + m)
                return carry

            lax.fori_loop(0, nvar * nvar, spread, 0, unroll=5)
        for i in range(len(JA_STEPS)):
            small_copy(it, i, True).wait_recv()
        for e in range(NX):
            for v in range(nvar):
                if e < NX - 1:
                    small_vec[e, v] = edge * unpack(small[it, e], v)
                if e > 0:
                    small_vec[e, nvar + v] = edge * unpack(small[it, e], nvar + v)
        low_end, high_end = pl.ds(0, nvar), pl.ds(nvar, nvar)
        x1 = small_vec[0, low_end]
        x2 = small_vec[1, low_end] + times(edge_mat[1, 0], x1)
        x3 = small_vec[2, low_end] + times(edge_mat[2, 0], x2)
        y2 = small_vec[3, high_end] + times(edge_mat[3, 2], x3)
        y1 = small_vec[2, high_end] + times(edge_mat[2, 2], x2) + times(edge_mat[2, 1], y2)
        y0 = small_vec[1, high_end] + times(edge_mat[1, 2], x1) + times(edge_mat[1, 1], y1)
        ghost_x[...] = jnp.where(ja == 0, 0.0, jnp.where(ja == 1, x1, jnp.where(ja == 2, x2, x3)))
        ghost_y[...] = jnp.where(ja == 3, 0.0, jnp.where(ja == 2, y2, jnp.where(ja == 1, y1, y0)))

        if it == 0:
            await_matrices(1, False)
            await_matrices(0, False)
        await_sweep(it, False)

        @pl.when(ja == 3)
        def _():
            yin[...] = jnp.zeros(vec, F32)

        @pl.when(ja == 2)
        def _():
            yin[...] = cy[it, 3]

        @pl.when(ja == 1)
        def _():
            yin[...] = cy[it, 2] + times(got_b[1], cy[it, 3])

        @pl.when(ja == 0)
        def _():
            yin[...] = cy[it, 1] + times(got_b[0], cy[it, 2] + times(got_b[1], cy[it, 3]))

        @pl.when(ja > 0)
        def _():
            halo_copy(it, True).wait_send()

        @pl.when(ja < NX - 1)
        def _():
            halo_copy(it, False).wait_send()

        xin[...] += ghost_x[...]
        yin[...] += ghost_y[...]

        def raise_plane(j, carry):
            cur[j] += sol[j] + times(hh[j], xin[...]) + times(rr[j], yin[...])
            return carry

        lax.fori_loop(0, planes, raise_plane, 0, unroll=2)
        if it < ITERS - 1:
            pack_faces(it + 1)

    for it in range(ITERS):
        for i in range(len(FACE_STEPS)):
            face_copy(it, i, False).wait_send()
        for dz in Z_STEPS:
            z_copy(it, dz).wait_send()
        for i in range(len(JA_STEPS)):
            small_copy(it, i, False).wait_send()
        for lower, pairs in ((True, LOWER_PAIRS), (False, UPPER_PAIRS)):
            for source, to, kind in pairs:
                @pl.when(ja == source)
                def _(source=source, to=to, kind=kind, lower=lower):
                    sweep_copy(it, source, to, kind, lower).wait_send()

    @pl.when(ja > 0)
    def _():
        for i in range(len(JA_STEPS)):
            edge_copy(i).wait_send()

    for lower, pairs in ((True, LOWER_MATS), (False, UPPER_MATS)):
        for e, to in pairs:
            @pl.when(ja == e)
            def _(e=e, to=to, lower=lower):
                matrix_copy(e, to, lower).wait_send()


def write_out(state_ref, resid_ref, state_out, resid_out, sems):
    copies = [
        pltpu.make_async_copy(state_ref, state_out, sems.at[0]),
        pltpu.make_async_copy(resid_ref, resid_out, sems.at[1]),
    ]
    for copy in copies:
        copy.start()
    for copy in copies:
        copy.wait()


def per_device(flow_state, forcing, diag_block, lower_jac, upper_jac, block_inv, east_zone, zone_depth):
    planes, nvar, depth_k, width = flow_state.shape[1:]
    tile = (depth_k, width)
    vec = (nvar,) + tile
    mat = (nvar,) + vec
    dma = pltpu.SemaphoreType.DMA

    def vmem(*shape):
        return pltpu.VMEM(shape, F32)

    ints = pltpu.SMEM(east_zone.shape, jnp.int32)
    state, resid = pl.pallas_call(
        kernel,
        out_shape=[pltpu.VMEM((planes,) + vec, F32)] * 2,
        in_specs=[pl.BlockSpec(memory_space=pltpu.HBM)] * 8,
        out_specs=[pl.BlockSpec(memory_space=pltpu.VMEM)] * 2,
        scratch_shapes=[ints, ints]
        + [vmem(planes, *vec)] + [vmem(planes, *mat)] * 4
        + [vmem(planes, *mat)] * 5 + [vmem(planes, *vec)] * 2 + [vmem(*mat), vmem(2, *mat)]
        + [vmem(NX, 2, *tile), vmem(NX, 3, *mat), vmem(2, NY, *tile), vmem(2, NY, *tile)]
        + [vmem(ITERS, NZ, *tile)] * 2 + [vmem(ITERS, 2, *vec)]
        + [vmem(ITERS, 2, *vec), vmem(ITERS, *vec)] + [vmem(ITERS, NX, *vec)] * 2 + [vmem(*vec)] * 4
        + [vmem(ITERS, NX, *tile), vmem(NX, 2 * nvar, *tile)]
        + [dma((8,)), dma((ITERS, 7)), dma((ITERS, 7)), dma((ITERS, NZ)), dma((ITERS, NZ)), dma((ITERS, 2)), dma((ITERS, 2))]
        + [dma((2,)), dma, dma((2,)), dma((2,)), dma((3,)), dma((3,))]
        + [dma((ITERS, NX))] * 4 + [dma((ITERS, 3))] * 2,
        compiler_params=pltpu.CompilerParams(
            collective_id=0, has_side_effects=True, vmem_limit_bytes=63 * 2**20),
        name="ssor",
    )(east_zone, zone_depth, flow_state[0], forcing[0], diag_block[0], lower_jac[0], upper_jac[0], block_inv[0])
    state, resid = pl.pallas_call(
        write_out,
        out_shape=[jax.ShapeDtypeStruct((planes,) + vec, F32)] * 2,
        in_specs=[pl.BlockSpec(memory_space=pltpu.VMEM)] * 2,
        out_specs=[pl.BlockSpec(memory_space=pltpu.HBM)] * 2,
        scratch_shapes=[dma((2,))],
        name="write_out",
    )(*(pltpu.with_memory_space_constraint(array, pltpu.VMEM) for array in (state, resid)))
    return state[None], resid[None]


def solution(mesh):
    vec = P("zone", "ja", None, None, None)
    mat = P("zone", "ja", None, None, None, None)
    return jax.shard_map(
        per_device,
        mesh=mesh,
        in_specs=(vec, vec, mat, mat, mat, mat, P(), P()),
        out_specs=(vec, vec),
        check_vma=False,
    )
```

```python
import jax
import jax.numpy as jnp
from jax import lax
from jax.experimental import pallas as pl
from jax.experimental.pallas import tpu as pltpu
from jax.sharding import PartitionSpec as P

ITERS = 2
OMEGA = 1.2
COUPLE = 0.25
NY, NZ, NX = 4, 8, 4
MESH = pl.DeviceIdType.MESH
F32 = jnp.float32
FACE_STEPS = ((2, 1), (2, 0), (1, 1), (3, 1), (1, 0), (3, 0), (0, 1))
Z_STEPS = (4, 3, 5, 2, 6, 1, 7)
JA_STEPS = (2, 1, 3)
LOWER_PAIRS = ((0, 2, 0), (1, 3, 0), (1, 2, 0), (2, 3, 0), (0, 1, 0), (0, 3, 1))
UPPER_PAIRS = ((3, 1, 0), (2, 0, 0), (3, 0, 0), (3, 2, 0), (2, 1, 0), (1, 0, 0))
LOWER_MATS = ((1, 0), (1, 2), (2, 3))
UPPER_MATS = ((2, 1), (1, 0), (2, 0))


def kernel(
    east_hbm, depth_hbm, flow_hbm, forc_hbm, diag_hbm, low_hbm, upp_hbm, inv_hbm,
    cur, res,
    east_ref, depth_ref, forc, diag, low, upp, inv,
    mm, nn, pp, rr, hh, gres, sol, got_a, got_b,
    edge_pack, edge_mat, face0, face1, chosen, ghost_in, halo,
    sb, sc, bx, cy, xin, yin, ghost_x, ghost_y, small, small_vec,
    load_sem, face_s, face_r, z_s, z_r, halo_s, halo_r,
    a_s, a_r, b_s, b_r, e_s, e_r, x_s, x_r, u_s, u_r, g_s, g_r,
):
    planes, nvar, depth_k, width = cur.shape
    rows = nvar * depth_k
    last = planes - 1
    vec = (nvar, depth_k, width)
    faces = (face0, face1)
    zone = lax.axis_index("zone")
    ja = lax.axis_index("ja")
    y, z, c = zone // (2 * NZ), (zone // 2) % NZ, zone % 2

    def at(dy, dz, flip):
        core = 1 - c if flip else c
        return (((y + dy) % NY) * (2 * NZ) + ((z + dz) % NZ) * 2 + core, ja)

    def along(dx):
        return (zone, (ja + dx) % NX)

    def on(device):
        return (zone, jnp.int32(device))

    barrier = pltpu.get_barrier_semaphore()
    partners = [at(dy, 0, flip) for dy, flip in FACE_STEPS] + [at(0, d, 0) for d in Z_STEPS]
    partners += [along(d) for d in JA_STEPS]
    for partner in partners:
        pl.semaphore_signal(barrier, 1, device_id=partner, device_id_type=MESH)

    sources = (
        (east_hbm, east_ref), (depth_hbm, depth_ref), (flow_hbm, cur), (inv_hbm, inv),
        (low_hbm, low), (upp_hbm, upp), (diag_hbm, diag), (forc_hbm, forc))
    loads = [pltpu.make_async_copy(src, dst, load_sem.at[i]) for i, (src, dst) in enumerate(sources)]
    for load in loads:
        load.start()

    k_index = lax.broadcasted_iota(jnp.int32, (depth_k, width), 0)
    lane = lax.broadcasted_iota(jnp.int32, (depth_k, width), 1)
    edge = ((lane == 0) | (lane == width - 1)).astype(F32)
    left_ok = (lane > 0).astype(F32)
    right_ok = (lane < width - 1).astype(F32)
    down_ok = (k_index > 0).astype(F32)
    up_ok = (k_index < depth_k - 1).astype(F32)
    odd = lane % 2 == 1

    def remote(src, dst, ss, rs, device):
        return pltpu.make_async_remote_copy(src, dst, ss, rs, device_id=device, device_id_type=MESH)

    def times(mat, v):
        out = mat[:, 0] * v[0][None]
        for col in range(1, nvar):
            out += mat[:, col] * v[col][None]
        return out

    def pack(tile, m, packet):
        turned = pltpu.roll(tile, 2 * m + 1, 1)
        return jnp.where((lane == 2 * m) | (lane == 2 * m + 1), turned, packet)

    def unpack(packet, m):
        return pltpu.roll(packet, width - 1 - 2 * m, 1)

    def pack_faces(it):
        packet = jnp.zeros((depth_k, width), F32)
        for m in range(planes * nvar):
            packet = pack(cur[m // nvar, m % nvar], m, packet)
        faces[it][c, y] = packet

    def face_copy(it, i, incoming):
        dy, flip = FACE_STEPS[i]
        slot = faces[it].at[1 - c if flip else c, (y - dy) % NY] if incoming else faces[it].at[c, y]
        return remote(faces[it].at[c, y], slot, face_s.at[it, i], face_r.at[it, i], at(dy, 0, flip))

    def z_copy(it, dz):
        return remote(chosen.at[it, dz], ghost_in.at[it, dz], z_s.at[it, dz], z_r.at[it, dz], at(0, dz, 0))

    def halo_copy(it, up):
        side = 1 if up else 0
        return remote(
            cur.at[0 if up else last], halo.at[it, side], halo_s.at[it, side], halo_r.at[it, side],
            along(NX - 1 if up else 1))

    def matrix_copy(e, to, lower):
        if lower:
            return remote(pp.at[last], got_a, a_s.at[to // 2], a_r, on(to))
        return remote(rr.at[0], got_b.at[e - 1], b_s.at[to], b_r.at[e - 1], on(to))

    def edge_copy(i):
        dx = JA_STEPS[i]
        return remote(edge_pack.at[ja], edge_pack.at[ja], e_s.at[i], e_r.at[i], along(dx))

    def edge_arrival(i):
        source = (ja - JA_STEPS[i]) % NX
        return remote(edge_pack.at[source], edge_pack.at[source], e_s.at[i], e_r.at[i], along(JA_STEPS[i]))

    def small_copy(it, i, incoming):
        dx = JA_STEPS[i]
        slot = (ja - dx) % NX if incoming else ja
        return remote(small.at[it, ja], small.at[it, slot], g_s.at[it, i], g_r.at[it, i], along(dx))

    def sweep_copy(it, source, to, through, lower):
        send = sb.at[it, through] if lower else sc.at[it]
        got, ss, rs = (bx, x_s, x_r) if lower else (cy, u_s, u_r)
        return remote(send, got.at[it, source], ss.at[it, to], rs.at[it, source], on(to))

    def send_matrices(lower):
        for e, to in LOWER_MATS if lower else UPPER_MATS:
            @pl.when(ja == e)
            def _(e=e, to=to):
                matrix_copy(e, to, lower).start()

    def await_matrices(device, lower):
        for e, to in LOWER_MATS if lower else UPPER_MATS:
            if to == device:
                @pl.when(ja == device)
                def _(e=e):
                    matrix_copy(e, device, lower).wait_recv()

    def send_sweep(it, through, lower):
        for source, to, kind in LOWER_PAIRS if lower else UPPER_PAIRS:
            if kind == through:
                @pl.when(ja == source)
                def _(source=source, to=to):
                    sweep_copy(it, source, to, through, lower).start()

    def await_sweep(it, lower):
        for source, to, kind in LOWER_PAIRS if lower else UPPER_PAIRS:
            @pl.when(ja == to)
            def _(source=source, to=to, kind=kind):
                sweep_copy(it, source, to, kind, lower).wait_recv()

    def residual_bulk(live):
        def step(j, below):
            here = cur[j]
            above = jnp.where(j == last, 0.0, cur[jnp.minimum(j + 1, last)])
            flat = here.reshape(rows, width)

            def shifted(by, axis, size, mask):
                return pltpu.roll(flat, by % size, axis).reshape(vec) * mask[None]

            beside = shifted(1, 1, width, left_ok) + shifted(-1, 1, width, right_ok)
            beside += shifted(1, 0, rows, down_ok) + shifted(-1, 0, rows, up_ok)
            applied = times(diag[j], here) - times(low[j], below) - times(upp[j], above) - COUPLE * beside
            res[j] = live[None] * (forc[j] - applied)
            return here

        lax.fori_loop(0, planes, step, jnp.zeros(vec, F32))

        def start(j, carry):
            sol[j] = times(inv[j], res[j])
            return carry

        lax.fori_loop(1, last, start, 0, unroll=2)

    loads[0].wait()
    loads[1].wait()
    targets = [at(0, d, 0)[0] for d in range(NZ)]

    def find(w, found):
        e = east_ref[w]
        return tuple(jnp.where(e == t, w, f) for t, f in zip(targets, found))

    wests = lax.fori_loop(0, NY * NZ * 2, find, (jnp.int32(0),) * NZ)
    easts = [east_ref[t] for t in targets]
    live = (k_index < depth_ref[zone]).astype(F32)
    ghost_weight = COUPLE * live * edge

    loads[2].wait()

    def mask_plane(j, carry):
        cur[j] = cur[j] * live[None]
        return carry

    lax.fori_loop(0, planes, mask_plane, 0, unroll=2)
    pack_faces(0)
    for i in (3, 4, 5):
        loads[i].wait()

    def premultiply(j, carry):
        for source, target in ((low, mm), (upp, nn)):
            for col in range(nvar):
                target[j, :, col] = OMEGA * times(inv[j], source[j, :, col])
        return carry

    lax.fori_loop(0, planes, premultiply, 0)
    pp[0] = mm[0]
    rr[last] = nn[last]

    def products(s, carry):
        j = last - s
        for col in range(nvar):
            pp[s, :, col] = times(mm[s], pp[s - 1, :, col])
            rr[j, :, col] = times(nn[j], rr[j + 1, :, col])
        return carry

    lax.fori_loop(1, planes, products, 0)
    hh[last] = pp[last]

    def through(s, carry):
        j = last - s
        for col in range(nvar):
            hh[j, :, col] = pp[j, :, col] + times(nn[j], hh[j + 1, :, col])
        return carry

    lax.fori_loop(1, planes, through, 0)
    packets = [jnp.zeros((depth_k, width), F32)] * 2
    for row in range(nvar):
        for col in range(nvar):
            m = row * nvar + col
            packets[0] = pack(pp[last, row, col], m, packets[0])
            packets[0] = pack(rr[0, row, col], nvar * nvar + m, packets[0])
            packets[1] = pack(hh[0, row, col], m, packets[1])
    for i in range(2):
        edge_pack[ja, i] = packets[i]
    loads[6].wait()
    loads[7].wait()
    residual_bulk(live)
    pl.semaphore_wait(barrier, len(partners))

    for it in range(ITERS):
        for i in range(len(FACE_STEPS)):
            face_copy(it, i, False).start()

        @pl.when(ja > 0)
        def _():
            halo_copy(it, True).start()

        @pl.when(ja < NX - 1)
        def _():
            halo_copy(it, False).start()

        if it == 0:
            send_matrices(True)
        else:
            residual_bulk(live)

        @pl.when(ja > 0)
        def _():
            halo_copy(it, False).wait_recv()
            res[0] += live[None] * times(low[0], halo[it, 0])

        @pl.when(ja < NX - 1)
        def _():
            halo_copy(it, True).wait_recv()
            res[last] += live[None] * times(upp[last], halo[it, 1])

        sol[0] = times(inv[0], res[0])
        sol[last] = times(inv[last], res[last])

        def through_lower(it):
            @pl.when(ja == 0)
            def _():
                sb[it, 1] = times(got_a, sb[it, 0])

            send_sweep(it, 1, True)

        def lower_step(j, before):
            value = sol[j] + times(mm[j], before)
            sol[j] = value
            return value

        def upper_step(s, after):
            j = last - s
            value = sol[j] + times(nn[j], after)
            sol[j] = value
            return value

        sb[it, 0] = lax.fori_loop(1, planes, lower_step, sol[0], unroll=True)
        send_sweep(it, 0, True)
        if it == 0:
            send_matrices(False)
            @pl.when(ja > 0)
            def _():
                for i in range(len(JA_STEPS)):
                    edge_copy(i).start()
        else:
            through_lower(it)
        sc[it] = lax.fori_loop(1, planes, upper_step, sol[last], unroll=True)

        for i in range(len(FACE_STEPS)):
            face_copy(it, i, True).wait_recv()
        for dz in Z_STEPS + (0,):
            w, e = wests[dz], easts[dz]
            west = faces[it][w % 2, w // (2 * NZ)]
            east = faces[it][e % 2, e // (2 * NZ)]
            west = jnp.where((w // 2) % NZ == z, west, 0.0)
            east = jnp.where((e // 2) % NZ == z, east, 0.0)
            chosen[it, dz] = jnp.where(odd, pltpu.roll(west, 1, 1), pltpu.roll(east, width - 1, 1))
            if dz:
                z_copy(it, dz).start()

        def lower_inflow():
            await_sweep(it, True)

            @pl.when(ja == 0)
            def _():
                xin[...] = jnp.zeros(vec, F32)

            @pl.when(ja == 1)
            def _():
                xin[...] = bx[it, 0]

            @pl.when(ja == 2)
            def _():
                xin[...] = bx[it, 1] + times(got_a, bx[it, 0])

            @pl.when(ja == 3)
            def _():
                xin[...] = bx[it, 2] + times(got_a, bx[it, 1] + bx[it, 0])

            sc[it] += times(hh[0], xin[...])
            send_sweep(it, 0, False)


        def ghost_response():
            for dz in Z_STEPS:
                z_copy(it, dz).wait_recv()
            ghosts = chosen[it, 0]
            for dz in Z_STEPS:
                ghosts += ghost_in[it, dz]
            bottom = None
            for j in range(planes):
                mine = [ghost_weight * unpack(ghosts, j * nvar + v) for v in range(nvar)]
                value = times(inv[j], mine)
                if j:
                    value += times(mm[j], bottom)
                gres[j] = value
                bottom = value
                for v in range(nvar):
                    res[j, v] += mine[v]

            def ghost_upper(s, after):
                j = last - s
                value = gres[j] + times(nn[j], after)
                sol[j] += value
                return value

            sol[last] += bottom
            top = lax.fori_loop(1, planes, ghost_upper, bottom, unroll=True)
            packet = jnp.zeros((depth_k, width), F32)
            for v in range(nvar):
                packet = pack(bottom[v], v, packet)
                packet = pack(top[v], nvar + v, packet)
            small[it, ja] = packet
            for i in range(len(JA_STEPS)):
                small_copy(it, i, False).start()


        if it == 0:
            await_matrices(0, True)
            through_lower(it)
            await_matrices(2, True)
            pl.when(ja < NX - 1)(lower_inflow)
            ghost_response()
            await_matrices(NX - 1, True)
            pl.when(ja == NX - 1)(lower_inflow)
        else:
            pl.when(ja < NX - 1)(lower_inflow)
            ghost_response()
            pl.when(ja == NX - 1)(lower_inflow)

        if it == 0:
            for i in range(len(JA_STEPS)):
                pl.when(ja != JA_STEPS[i])(edge_arrival(i).wait_recv)

            def spread(m, carry):
                row, col = m // nvar, m % nvar
                for e in (1, 2, 3):
                    edge_mat[e, 2, row, col] = unpack(edge_pack[e, 1], m)
                    if e < 3:
                        edge_mat[e, 0, row, col] = unpack(edge_pack[e, 0], m)
                        edge_mat[e, 1, row, col] = unpack(edge_pack[e, 0], nvar * nvar + m)
                return carry

            lax.fori_loop(0, nvar * nvar, spread, 0, unroll=5)
        for i in range(len(JA_STEPS)):
            small_copy(it, i, True).wait_recv()
        for e in range(NX):
            for v in range(nvar):
                if e < NX - 1:
                    small_vec[e, v] = edge * unpack(small[it, e], v)
                if e > 0:
                    small_vec[e, nvar + v] = edge * unpack(small[it, e], nvar + v)
        low_end, high_end = pl.ds(0, nvar), pl.ds(nvar, nvar)
        x1 = small_vec[0, low_end]
        x2 = small_vec[1, low_end] + times(edge_mat[1, 0], x1)
        x3 = small_vec[2, low_end] + times(edge_mat[2, 0], x2)
        y2 = small_vec[3, high_end] + times(edge_mat[3, 2], x3)
        y1 = small_vec[2, high_end] + times(edge_mat[2, 2], x2) + times(edge_mat[2, 1], y2)
        y0 = small_vec[1, high_end] + times(edge_mat[1, 2], x1) + times(edge_mat[1, 1], y1)
        ghost_x[...] = jnp.where(ja == 0, 0.0, jnp.where(ja == 1, x1, jnp.where(ja == 2, x2, x3)))
        ghost_y[...] = jnp.where(ja == 3, 0.0, jnp.where(ja == 2, y2, jnp.where(ja == 1, y1, y0)))

        if it == 0:
            await_matrices(1, False)
            await_matrices(0, False)
        await_sweep(it, False)

        @pl.when(ja == 3)
        def _():
            yin[...] = jnp.zeros(vec, F32)

        @pl.when(ja == 2)
        def _():
            yin[...] = cy[it, 3]

        @pl.when(ja == 1)
        def _():
            yin[...] = cy[it, 2] + times(got_b[1], cy[it, 3])

        @pl.when(ja == 0)
        def _():
            yin[...] = cy[it, 1] + times(got_b[0], cy[it, 2] + times(got_b[1], cy[it, 3]))

        @pl.when(ja > 0)
        def _():
            halo_copy(it, True).wait_send()

        @pl.when(ja < NX - 1)
        def _():
            halo_copy(it, False).wait_send()

        inflow = xin[...] + ghost_x[...]
        backflow = yin[...] + ghost_y[...]
        packet = jnp.zeros((depth_k, width), F32)
        for j in range(planes):
            value = cur[j] + sol[j] + times(hh[j], inflow) + times(rr[j], backflow)
            cur[j] = value
            if it < ITERS - 1:
                for v in range(nvar):
                    packet = pack(value[v], j * nvar + v, packet)
        if it < ITERS - 1:
            faces[it + 1][c, y] = packet

    for it in range(ITERS):
        for i in range(len(FACE_STEPS)):
            face_copy(it, i, False).wait_send()
        for dz in Z_STEPS:
            z_copy(it, dz).wait_send()
        for i in range(len(JA_STEPS)):
            small_copy(it, i, False).wait_send()
        for lower, pairs in ((True, LOWER_PAIRS), (False, UPPER_PAIRS)):
            for source, to, kind in pairs:
                @pl.when(ja == source)
                def _(source=source, to=to, kind=kind, lower=lower):
                    sweep_copy(it, source, to, kind, lower).wait_send()

    @pl.when(ja > 0)
    def _():
        for i in range(len(JA_STEPS)):
            edge_copy(i).wait_send()

    for lower, pairs in ((True, LOWER_MATS), (False, UPPER_MATS)):
        for e, to in pairs:
            @pl.when(ja == e)
            def _(e=e, to=to, lower=lower):
                matrix_copy(e, to, lower).wait_send()


def write_out(state_ref, resid_ref, state_out, resid_out, sems):
    copies = [
        pltpu.make_async_copy(state_ref, state_out, sems.at[0]),
        pltpu.make_async_copy(resid_ref, resid_out, sems.at[1]),
    ]
    for copy in copies:
        copy.start()
    for copy in copies:
        copy.wait()


def per_device(flow_state, forcing, diag_block, lower_jac, upper_jac, block_inv, east_zone, zone_depth):
    planes, nvar, depth_k, width = flow_state.shape[1:]
    tile = (depth_k, width)
    vec = (nvar,) + tile
    mat = (nvar,) + vec
    dma = pltpu.SemaphoreType.DMA

    def vmem(*shape):
        return pltpu.VMEM(shape, F32)

    ints = pltpu.SMEM(east_zone.shape, jnp.int32)
    state, resid = pl.pallas_call(
        kernel,
        out_shape=[pltpu.VMEM((planes,) + vec, F32)] * 2,
        in_specs=[pl.BlockSpec(memory_space=pltpu.HBM)] * 8,
        out_specs=[pl.BlockSpec(memory_space=pltpu.VMEM)] * 2,
        scratch_shapes=[ints, ints]
        + [vmem(planes, *vec)] + [vmem(planes, *mat)] * 4
        + [vmem(planes, *mat)] * 5 + [vmem(planes, *vec)] * 2 + [vmem(*mat), vmem(2, *mat)]
        + [vmem(NX, 2, *tile), vmem(NX, 3, *mat), vmem(2, NY, *tile), vmem(2, NY, *tile)]
        + [vmem(ITERS, NZ, *tile)] * 2 + [vmem(ITERS, 2, *vec)]
        + [vmem(ITERS, 2, *vec), vmem(ITERS, *vec)] + [vmem(ITERS, NX, *vec)] * 2 + [vmem(*vec)] * 4
        + [vmem(ITERS, NX, *tile), vmem(NX, 2 * nvar, *tile)]
        + [dma((8,)), dma((ITERS, 7)), dma((ITERS, 7)), dma((ITERS, NZ)), dma((ITERS, NZ)), dma((ITERS, 2)), dma((ITERS, 2))]
        + [dma((2,)), dma, dma((2,)), dma((2,)), dma((3,)), dma((3,))]
        + [dma((ITERS, NX))] * 4 + [dma((ITERS, 3))] * 2,
        compiler_params=pltpu.CompilerParams(
            collective_id=0, has_side_effects=True, vmem_limit_bytes=63 * 2**20),
        name="ssor",
    )(east_zone, zone_depth, flow_state[0], forcing[0], diag_block[0], lower_jac[0], upper_jac[0], block_inv[0])
    state, resid = pl.pallas_call(
        write_out,
        out_shape=[jax.ShapeDtypeStruct((planes,) + vec, F32)] * 2,
        in_specs=[pl.BlockSpec(memory_space=pltpu.VMEM)] * 2,
        out_specs=[pl.BlockSpec(memory_space=pltpu.HBM)] * 2,
        scratch_shapes=[dma((2,))],
        name="write_out",
    )(*(pltpu.with_memory_space_constraint(array, pltpu.VMEM) for array in (state, resid)))
    return state[None], resid[None]


def solution(mesh):
    vec = P("zone", "ja", None, None, None)
    mat = P("zone", "ja", None, None, None, None)
    return jax.shard_map(
        per_device,
        mesh=mesh,
        in_specs=(vec, vec, mat, mat, mat, mat, P(), P()),
        out_specs=(vec, vec),
        check_vma=False,
    )
```
